32 devices in a mesh: rep: 8 (over z, y), tp: 4 (over x, core).
Axes of the slice: x: 2, y: 2, z: 4, core: 2. Of those that a mesh axis runs over, the one named last changes fastest.
Arguments:
- gradients: bfloat16 [8, 1024, 1024], P('rep', None, 'tp'), may hold values from -6 to 6
- feedback: float32 [8, 1024, 1024], P('rep', None, 'tp'), may hold values from -4 to 4
- warm_factor: float32 [1024, 32], P('tp'), may hold values from -0.1875 to 0.1875
- momentum: float32 [1024, 1024], P('rep', 'tp'), may hold values from -3 to 3
- master_owned: float32 [1024, 1024], P('rep', 'tp'), may hold values from -4 to 4
- vector_grads: float32 [8, 2560], P('rep'), may hold values from -6 to 6
- vector_params: float32 [2560], replicated, may hold values from 0.5 to 1.5
- vector_momentum: float32 [2560], replicated, may hold values from -3 to 3
Outputs:
- new_feedback: float32 [8, 1024, 1024], P('rep', None, 'tp')
- new_momentum: float32 [1024, 1024], P('rep', 'tp')
- new_master: float32 [1024, 1024], P('rep', 'tp')
- weight: bfloat16 [1024, 1024], P(None, 'tp')
- new_vector_params: float32 [2560], replicated
- new_vector_momentum: float32 [2560], replicated
The draws below stay inside these ranges and needn't reach their ends.
All inputs are finite; a program needn't handle non-finite values.
Results may differ from the reference program's by a relative error of at most 0.0049.
Values may be sent and summed in bfloat16 or wider, within the bound.
A program may use at most 64 MiB of HBM per device.

```python
import jax
import jax.numpy as jnp
from jax import lax

D = 1024
RANK = 32
REPLICAS = 8
VEC = 2560


def with_spikes(drawn, rng, source, target, shards_of, factor):
    owner, partner = [(jnp.arange(drawn.shape[dim]) // (drawn.shape[dim] // shards_of)).reshape([-1 if axis == dim else 1 for axis in range(drawn.ndim)]) for dim in (source, target)]
    chosen = jax.random.permutation(rng, shards_of)[partner]
    strong = (owner == chosen) | (owner == (partner + shards_of // 2) % shards_of)
    return jnp.where(strong, factor * drawn, drawn)


def block_scale(own_key, extent, cuts, low, high):
    def one(position, shards_of):
        steps = jax.random.uniform(jax.random.fold_in(jax.random.fold_in(own_key, 6), position), (shards_of,), jnp.float32, low / len(cuts), high / len(cuts))
        return jnp.repeat(jnp.exp(steps), extent[position] // shards_of).reshape((-1,) + (1,) * (len(extent) - position - 1))

    gain = one(*cuts[0])
    for cut in cuts[1:]:
        gain = gain * one(*cut)
    return gain


def normal_values(own_key, shape, width, bound, cuts=(), kind=jnp.bfloat16):
    factor_of = block_scale(own_key, shape, cuts, -0.22, 0.18) if cuts else 1.0
    drawn = jax.random.normal(own_key, shape, jnp.float32) * width * factor_of
    return jnp.minimum(jnp.maximum(drawn, -bound), bound).astype(kind)


def noise_with(rng, shape, width, reach, cuts, heavy, kind=jnp.bfloat16):
    array = width * jax.random.normal(rng, shape, jnp.float32)
    if cuts:
        array = array * block_scale(rng, shape, cuts, -0.22, 0.18)
    return jnp.clip(with_spikes(array, jax.random.fold_in(rng, 3), *heavy), -reach, reach).astype(kind)


def setup_inputs(seed: int = 0) -> dict:
    key_of = jax.random.split(jax.random.key(seed), 9)
    gradients = noise_with(key_of[0], (REPLICAS, D, D), 1.0, 6.0, ((0, 8), (2, 4)), (0, 1, 8, 2.0))
    feedback = normal_values(key_of[1], (REPLICAS, D, D), 0.5, 4.0, ((0, 8), (2, 4)), jnp.float32)
    warm_factor = normal_values(key_of[2], (D, RANK), D ** -0.5, 0.1875, ((0, 4),), jnp.float32)
    momentum = normal_values(key_of[3], (D, D), 0.3, 3.0, ((0, 8), (1, 4)), jnp.float32)
    master_owned = normal_values(key_of[4], (D, D), 0.5, 4.0, ((0, 8), (1, 4)), jnp.float32)
    vector_grads = normal_values(key_of[5], (REPLICAS, VEC), 1.0, 6.0, ((0, 8),), jnp.float32)
    vector_params = jnp.clip(1.0 + 0.1 * jax.random.normal(key_of[6], (VEC,), jnp.float32), 0.5, 1.5)
    vector_momentum = normal_values(key_of[7], (VEC,), 0.3, 3.0, (), jnp.float32)
    return dict(gradients=gradients, feedback=feedback, warm_factor=warm_factor, momentum=momentum, master_owned=master_owned, vector_grads=vector_grads, vector_params=vector_params, vector_momentum=vector_momentum)


PRECISE = lax.Precision.HIGHEST
MOMENTUM_RATE = 0.9
LEARN_RATE = 0.5

def combined_member(gradients, feedback, member):
    return gradients[member].astype(jnp.float32) + feedback[member]

def left_product(gradients, feedback, factor):

    def accumulate(total, member):
        part = jnp.dot(combined_member(gradients, feedback, member), factor, precision=PRECISE)
        return (total + part, None)
    total, unused = lax.scan(accumulate, jnp.zeros((D, RANK), jnp.float32), jnp.arange(REPLICAS, dtype=jnp.int32))
    return total

def right_product(gradients, feedback, factor):

    def accumulate(total, member):
        part = jnp.dot(combined_member(gradients, feedback, member).T, factor, precision=PRECISE)
        return (total + part, None)
    total, unused = lax.scan(accumulate, jnp.zeros((D, RANK), jnp.float32), jnp.arange(REPLICAS, dtype=jnp.int32))
    return total

def orthonormal(left):
    gram = jnp.dot(left.T, left, precision=PRECISE)
    lower = jnp.linalg.cholesky(gram)
    return jax.scipy.linalg.solve_triangular(lower, left.T, lower=True).T

def reference(gradients, feedback, warm_factor, momentum, master_owned, vector_grads, vector_params, vector_momentum):
    left_one = left_product(gradients, feedback, warm_factor)
    ortho_one = orthonormal(left_one)
    right_one = right_product(gradients, feedback, ortho_one)
    left_two = left_product(gradients, feedback, right_one)
    ortho_two = orthonormal(left_two)
    right_two = right_product(gradients, feedback, ortho_two)
    approx = jnp.dot(ortho_two, right_two.T, precision=PRECISE) / REPLICAS
    new_feedback = gradients.astype(jnp.float32) + feedback - approx[None]
    new_momentum = MOMENTUM_RATE * momentum + approx
    new_master = master_owned - LEARN_RATE * new_momentum
    weight = new_master.astype(jnp.bfloat16)
    vector_sum = jnp.sum(vector_grads, axis=0)
    new_vector_momentum = MOMENTUM_RATE * vector_momentum + vector_sum / REPLICAS
    new_vector_params = vector_params - LEARN_RATE * new_vector_momentum
    return (new_feedback, new_momentum, new_master, weight, new_vector_params, new_vector_momentum)
```

```python
import functools

import jax
import jax.numpy as jnp
from jax import lax
from jax.experimental import pallas as pl
from jax.experimental.pallas import tpu as pltpu
from jax.sharding import PartitionSpec as P

PRECISE = lax.Precision.HIGHEST
MOMENTUM_RATE = 0.9
LEARN_RATE = 0.5


def left_factor(combined, factor):
    partial_terms = jnp.dot(combined, factor, precision=PRECISE)
    return lax.psum(partial_terms, ("rep", "tp"))


def orthonormal(left):
    gram = jnp.dot(left.T, left, precision=PRECISE)
    lower = jnp.linalg.cholesky(gram)
    return jax.scipy.linalg.solve_triangular(lower, left.T, lower=True).T


def right_terms(combined, ortho):
    return lax.dot_general(combined, ortho, (((0,), (0,)), ((), ())), precision=PRECISE)


def shards(
    gradients,
    feedback,
    warm_factor,
    momentum,
    master_owned,
    vector_grads,
    vector_params,
    vector_momentum,
):
    replicas = lax.axis_size("rep")
    combined = gradients[0].astype(jnp.float32) + feedback[0]
    vector_sum = lax.psum(vector_grads[0], "rep")
    left_one = left_factor(combined, warm_factor)
    ortho_one = orthonormal(left_one)
    right_one = lax.psum(right_terms(combined, ortho_one), "rep")
    left_two = left_factor(combined, right_one)
    ortho_two = orthonormal(left_two)
    right_two = lax.psum(right_terms(combined, ortho_two), "rep")
    approx = jnp.dot(ortho_two, right_two.T, precision=PRECISE) / replicas
    new_feedback = (combined - approx)[None]
    owned_rows = momentum.shape[0]
    row_start = lax.axis_index("rep") * owned_rows
    owned_approx = lax.dynamic_slice_in_dim(approx, row_start, owned_rows, 0)
    new_momentum = MOMENTUM_RATE * momentum + owned_approx
    new_master = master_owned - LEARN_RATE * new_momentum
    weight = lax.all_gather(new_master.astype(jnp.bfloat16), "rep", axis=0, tiled=True)
    new_vector_momentum = MOMENTUM_RATE * vector_momentum + vector_sum / replicas
    new_vector_params = vector_params - LEARN_RATE * new_vector_momentum
    return (new_feedback, new_momentum, new_master, weight, new_vector_params, new_vector_momentum)


LANES = 128
SUBLANES = 8
NT = (((1,), (1,)), ((), ()))
NN = (((1,), (0,)), ((), ()))
TN = (((0,), (0,)), ((), ()))


def dot16(a, b, dims):
    return lax.dot_general(a, b, dims, preferred_element_type=jnp.float32)


def split(x):
    high = x.astype(jnp.bfloat16)
    return high, (x - high.astype(jnp.float32)).astype(jnp.bfloat16)


def times_parts(a, high, low, dims):
    a_high, a_low = split(a)
    rank = a.shape[0]
    both = dot16(jnp.concatenate([a_high, a_low], axis=0), high, dims)
    return both[:rank] + both[rank:] + dot16(a_high, low, dims)


def gram_of(left_t):
    rank = left_t.shape[0]
    high, rest = left_t.astype(jnp.bfloat16), None
    rest = left_t - high.astype(jnp.float32)
    middle = rest.astype(jnp.bfloat16)
    low = (rest - middle.astype(jnp.float32)).astype(jnp.bfloat16)
    parts = jnp.concatenate([high, middle, low], axis=0)
    grid = dot16(parts, parts, NT)
    rows = grid[:rank] + grid[rank : 2 * rank] + grid[2 * rank :]
    return rows[:, :rank] + rows[:, rank : 2 * rank] + rows[:, 2 * rank :]


def inverse_lower(gram):
    rank = gram.shape[0]
    row_id = lax.broadcasted_iota(jnp.int32, (rank, 2 * rank), 0)
    lane_id = lax.broadcasted_iota(jnp.int32, (rank, 2 * rank), 1)
    unit = (lane_id == row_id + rank).astype(jnp.float32)
    work = jnp.concatenate([gram, unit[:, rank:]], axis=1)
    for j in range(rank):
        scale = lax.rsqrt(work[j : j + 1, j : j + 1])
        row = work[j : j + 1, :] * scale
        column = work[:, j : j + 1] * scale
        work = jnp.where(row_id < j, work, jnp.where(row_id == j, row, work - column * row))
    return work[:, rank:]


def step_kernel(
    reps,
    tps,
    grad_ref,
    feed_ref,
    warm_ref,
    mom_ref,
    master_ref,
    vgrad_ref,
    vpar_ref,
    vmom_ref,
    new_feed_ref,
    new_mom_ref,
    new_master_ref,
    weight_ref,
    new_vpar_ref,
    new_vmom_ref,
    pair_send,
    pair_recv,
    line_send,
    line_recv,
    base_all,
    tp_send,
    tp_recv,
    left_all,
    piece_send,
    piece_recv,
    right_all,
    vec_all,
    ortho_parts,
    pair_ss,
    pair_rs,
    line_ss,
    line_rs,
    base_ss,
    base_rs,
    fwd_ss,
    fwd_rs,
    tp_ss,
    tp_rs,
    left_ss,
    left_rs,
    piece_ss,
    piece_rs,
    right_ss,
    right_rs,
    vec_ss,
    vec_rs,
):
    me = lax.axis_index("rep")
    col = lax.axis_index("tp")
    lines = reps // 2
    far, near = me // 2, me % 2
    partner = far * 2 + (1 - near)
    rows, cols = mom_ref.shape
    rank = warm_ref.shape[1]
    half = rank // SUBLANES

    def rep_peer(k):
        return lax.rem(me + k, reps)

    def tp_peer(k):
        return lax.rem(col + k, tps)

    def line_at(d):
        return lax.rem(far + d, lines)

    def send(src, dst, ss, rs, peer):
        copy = pltpu.make_async_remote_copy(
            src_ref=src, dst_ref=dst, send_sem=ss, recv_sem=rs,
            device_id=peer, device_id_type=pl.DeviceIdType.MESH,
        )
        copy.start()
        sent.append(copy)
        return copy

    sent = []

    barrier = pltpu.get_barrier_semaphore()
    for k in range(1, reps):
        pl.semaphore_signal(barrier, inc=1, device_id={"rep": rep_peer(k)}, device_id_type=pl.DeviceIdType.MESH)
    for k in range(1, tps):
        pl.semaphore_signal(barrier, inc=1, device_id={"tp": tp_peer(k)}, device_id_type=pl.DeviceIdType.MESH)

    def combined_block(owner):
        at = pl.ds(pl.multiple_of(owner * rows, rows), rows)
        return grad_ref[at, :].astype(jnp.float32) + feed_ref[at, :]

    order = list(range(1, lines)) + [0]
    for d in order:
        pair_send[d] = combined_block(line_at(d) * 2 + (1 - near)).astype(jnp.bfloat16)
    base_all[me] = (master_ref[...] - (LEARN_RATE * MOMENTUM_RATE) * mom_ref[...]).astype(jnp.bfloat16)
    vec_all[me] = vgrad_ref[...]
    pl.semaphore_wait(barrier, reps - 1 + tps - 1)

    pairs = {}
    for d in order:
        pairs[d] = send(pair_send.at[d], pair_recv.at[d], pair_ss.at[d], pair_rs.at[d], {"rep": partner})
    line_copies = []
    for d in range(1, lines):
        mine = combined_block(line_at(d) * 2 + near)
        pairs[d].wait_recv()
        line_send[d] = (mine + pair_recv[d].astype(jnp.float32)).astype(jnp.bfloat16)
        line_copies.append(
            send(line_send.at[d], line_recv.at[d], line_ss.at[d], line_rs.at[d], {"rep": line_at(d) * 2 + near})
        )
    base_copies = [None]
    for d in range(1, lines):
        base_copies.append(
            send(base_all.at[me], base_all.at[me], base_ss.at[d], base_rs.at[d], {"rep": line_at(d) * 2 + near})
        )
    fwd_copies = [send(base_all.at[me], base_all.at[me], fwd_ss.at[0], fwd_rs.at[0], {"rep": partner})]
    vec_copies = []
    for k in range(1, reps):
        vec_copies.append(send(vec_all.at[me], vec_all.at[me], vec_ss.at[k], vec_rs.at[k], {"rep": rep_peer(k)}))
    warm_t = warm_ref[...].T
    total = combined_block(me)
    pairs[0].wait_recv()
    total = total + pair_recv[0].astype(jnp.float32)
    for d in range(1, lines):
        line_copies[d - 1].wait_recv()
        total = total + line_recv[d].astype(jnp.float32)
    sum_high, sum_low = split(total)

    def left_total(phase, factor_t):
        part = times_parts(factor_t, sum_high, sum_low, NT)
        tp_send[phase] = part
        copies = []
        for k in range(1, tps):
            copies.append(
                send(tp_send.at[phase], tp_recv.at[phase, k], tp_ss.at[phase, k], tp_rs.at[phase, k], {"tp": tp_peer(k)})
            )
        for k in range(1, tps):
            copies[k - 1].wait_recv()
            part = part + tp_recv[phase, k]
        return part

    def right_total(phase, left_t):
        left_all[phase, me] = left_t
        right_t = times_parts(left_t, sum_high, sum_low, NN)
        for s in range(cols // LANES):
            for q in range(half):
                piece_send[phase, s * half + q] = right_t[
                    q * SUBLANES : (q + 1) * SUBLANES, s * LANES : (s + 1) * LANES
                ]
        pieces, lefts, rights = [], [], []
        for k in range(1, reps):
            pieces.append(
                send(
                    piece_send.at[phase, rep_peer(k)], piece_recv.at[phase, k],
                    piece_ss.at[phase, k], piece_rs.at[phase, k], {"rep": rep_peer(k)},
                )
            )
        for k in range(1, reps):
            lefts.append(
                send(
                    left_all.at[phase, me], left_all.at[phase, me],
                    left_ss.at[phase, k], left_rs.at[phase, k], {"rep": rep_peer(k)},
                )
            )
        piece = piece_send[phase, me]
        for k in range(1, reps):
            pieces[k - 1].wait_recv()
            piece = piece + piece_recv[phase, k]
        right_all[phase, me] = piece
        for k in range(1, reps):
            rights.append(
                send(
                    right_all.at[phase, me], right_all.at[phase, me],
                    right_ss.at[phase, k], right_rs.at[phase, k], {"rep": rep_peer(k)},
                )
            )
        for copy in lefts:
            copy.wait_recv()
        left_full = jnp.concatenate([left_all[phase, r] for r in range(reps)], axis=1)
        unlower = inverse_lower(gram_of(left_full))

        def finish():
            for copy in rights:
                copy.wait_recv()
            raw = jnp.concatenate(
                [
                    jnp.concatenate([right_all[phase, s * half + q] for q in range(half)], axis=0)
                    for s in range(cols // LANES)
                ],
                axis=1,
            )
            return jnp.dot(unlower, raw, precision=PRECISE, preferred_element_type=jnp.float32)

        return left_full, unlower, finish

    left_one = left_total(0, warm_t)
    _, _, finish_one = right_total(0, left_one)
    right_one = finish_one()
    for d in range(1, lines):
        base_copies[d].wait_recv()
        slot = lax.rem(far + lines - d, lines) * 2 + near
        fwd_copies.append(send(base_all.at[slot], base_all.at[slot], fwd_ss.at[d], fwd_rs.at[d], {"rep": partner}))
    left_two = left_total(1, right_one)
    left_full, unlower, finish_two = right_total(1, left_two)
    un_high, un_low = split(unlower)
    left_high, left_low = split(left_full)
    ortho = dot16(
        jnp.concatenate([un_high, un_low, un_high], axis=1),
        jnp.concatenate([left_high, left_high, left_low], axis=0),
        NN,
    )
    ortho_high, ortho_low = split(ortho)
    ortho_cat = jnp.concatenate([ortho_high, ortho_low, ortho_high], axis=0)
    for r in range(reps):
        ortho_parts[r] = ortho_cat[:, r * rows : (r + 1) * rows]

    for copy in vec_copies:
        copy.wait_recv()
    vec_sum = vec_all[0]
    for r in range(1, reps):
        vec_sum = vec_sum + vec_all[r]
    vec_mom = MOMENTUM_RATE * vmom_ref[...] + vec_sum / reps
    new_vmom_ref[...] = vec_mom
    new_vpar_ref[...] = vpar_ref[...] - LEARN_RATE * vec_mom
    for copy in fwd_copies:
        copy.wait_recv()

    right_high, right_low = split(finish_two() / reps)
    right_cat = jnp.concatenate([right_high, right_high, right_low], axis=0)
    for r in range(reps):
        at = slice(r * rows, (r + 1) * rows)
        approx = dot16(ortho_parts[r], right_cat, TN)
        new_feed_ref[at, :] = grad_ref[at, :].astype(jnp.float32) + feed_ref[at, :] - approx
        weight_ref[at, :] = (base_all[r].astype(jnp.float32) - LEARN_RATE * approx).astype(jnp.bfloat16)
    own = dot16(ortho_parts[me], right_cat, TN)
    momentum = MOMENTUM_RATE * mom_ref[...] + own
    new_mom_ref[...] = momentum
    new_master_ref[...] = master_ref[...] - LEARN_RATE * momentum
    for copy in sent:
        copy.wait_send()


def kernel_shards(
    reps, tps, gradients, feedback, warm_factor, momentum, master_owned, vector_grads, vector_params, vector_momentum
):
    rows, cols = momentum.shape
    rank = warm_factor.shape[1]
    vec = vector_params.shape[0]
    lines = reps // 2
    f32, bf16 = jnp.float32, jnp.bfloat16
    dma = pltpu.SemaphoreType.DMA
    vmem = pl.BlockSpec(memory_space=pltpu.VMEM)
    outs = pl.pallas_call(
        functools.partial(step_kernel, reps, tps),
        out_shape=(
            jax.ShapeDtypeStruct(feedback.shape[1:], f32),
            jax.ShapeDtypeStruct((rows, cols), f32),
            jax.ShapeDtypeStruct((rows, cols), f32),
            jax.ShapeDtypeStruct(feedback.shape[1:], bf16),
            jax.ShapeDtypeStruct((1, vec), f32),
            jax.ShapeDtypeStruct((1, vec), f32),
        ),
        in_specs=[vmem] * 8,
        out_specs=(vmem,) * 6,
        scratch_shapes=[
            pltpu.VMEM((lines, rows, cols), bf16),
            pltpu.VMEM((lines, rows, cols), bf16),
            pltpu.VMEM((lines, rows, cols), bf16),
            pltpu.VMEM((lines, rows, cols), bf16),
            pltpu.VMEM((reps, rows, cols), bf16),
            pltpu.VMEM((2, rank, rows), f32),
            pltpu.VMEM((2, tps, rank, rows), f32),
            pltpu.VMEM((2, reps, rank, rows), f32),
            pltpu.VMEM((2, reps, SUBLANES, LANES), f32),
            pltpu.VMEM((2, reps, SUBLANES, LANES), f32),
            pltpu.VMEM((2, reps, SUBLANES, LANES), f32),
            pltpu.VMEM((reps, 1, vec), f32),
            pltpu.VMEM((reps, 3 * rank, rows), bf16),
            dma((lines,)), dma((lines,)),
            dma((lines,)), dma((lines,)),
            dma((lines,)), dma((lines,)),
            dma((lines,)), dma((lines,)),
            dma((2, tps)), dma((2, tps)),
            dma((2, reps)), dma((2, reps)),
            dma((2, reps)), dma((2, reps)),
            dma((2, reps)), dma((2, reps)),
            dma((reps,)), dma((reps,)),
        ],
        compiler_params=pltpu.CompilerParams(
            collective_id=0, has_side_effects=True, vmem_limit_bytes=40 * 1024 * 1024
        ),
    )(
        gradients[0], feedback[0], warm_factor, momentum, master_owned,
        vector_grads, vector_params[None], vector_momentum[None],
    )
    new_feedback, new_momentum, new_master, weight, new_params, new_vmom = outs
    return (new_feedback[None], new_momentum, new_master, weight, new_params[0], new_vmom[0])


def step(reps, tps, *arrays):
    rows, cols = arrays[3].shape
    rank = arrays[2].shape[1]
    pieces = (cols // LANES) * (rank // SUBLANES)
    if reps == pieces and reps % 2 == 0 and rows == LANES:
        return kernel_shards(reps, tps, *arrays)
    return shards(*arrays)


def solution(mesh):
    return jax.shard_map(
        functools.partial(step, mesh.shape["rep"], mesh.shape["tp"]),
        mesh=mesh,
        in_specs=(
            P("rep", None, "tp"),
            P("rep", None, "tp"),
            P("tp", None),
            P("rep", "tp"),
            P("rep", "tp"),
            P("rep", None),
            P(),
            P(),
        ),
        out_specs=(P("rep", None, "tp"), P("rep", "tp"), P("rep", "tp"), P(None, "tp"), P(), P()),
        check_vma=False,
    )
```

```python
import functools

import jax
import jax.numpy as jnp
from jax import lax
from jax.experimental import pallas as pl
from jax.experimental.pallas import tpu as pltpu
from jax.sharding import PartitionSpec as P

PRECISE = lax.Precision.HIGHEST
MOMENTUM_RATE = 0.9
LEARN_RATE = 0.5


def left_factor(combined, factor):
    partial_terms = jnp.dot(combined, factor, precision=PRECISE)
    return lax.psum(partial_terms, ("rep", "tp"))


def orthonormal(left):
    gram = jnp.dot(left.T, left, precision=PRECISE)
    lower = jnp.linalg.cholesky(gram)
    return jax.scipy.linalg.solve_triangular(lower, left.T, lower=True).T


def right_terms(combined, ortho):
    return lax.dot_general(combined, ortho, (((0,), (0,)), ((), ())), precision=PRECISE)


def shards(
    gradients,
    feedback,
    warm_factor,
    momentum,
    master_owned,
    vector_grads,
    vector_params,
    vector_momentum,
):
    replicas = lax.axis_size("rep")
    combined = gradients[0].astype(jnp.float32) + feedback[0]
    vector_sum = lax.psum(vector_grads[0], "rep")
    left_one = left_factor(combined, warm_factor)
    ortho_one = orthonormal(left_one)
    right_one = lax.psum(right_terms(combined, ortho_one), "rep")
    left_two = left_factor(combined, right_one)
    ortho_two = orthonormal(left_two)
    right_two = lax.psum(right_terms(combined, ortho_two), "rep")
    approx = jnp.dot(ortho_two, right_two.T, precision=PRECISE) / replicas
    new_feedback = (combined - approx)[None]
    owned_rows = momentum.shape[0]
    row_start = lax.axis_index("rep") * owned_rows
    owned_approx = lax.dynamic_slice_in_dim(approx, row_start, owned_rows, 0)
    new_momentum = MOMENTUM_RATE * momentum + owned_approx
    new_master = master_owned - LEARN_RATE * new_momentum
    weight = lax.all_gather(new_master.astype(jnp.bfloat16), "rep", axis=0, tiled=True)
    new_vector_momentum = MOMENTUM_RATE * vector_momentum + vector_sum / replicas
    new_vector_params = vector_params - LEARN_RATE * new_vector_momentum
    return (new_feedback, new_momentum, new_master, weight, new_vector_params, new_vector_momentum)


LANES = 128
SUBLANES = 8
NT = (((1,), (1,)), ((), ()))
NN = (((1,), (0,)), ((), ()))
TN = (((0,), (0,)), ((), ()))


def dot16(a, b, dims):
    return lax.dot_general(a, b, dims, preferred_element_type=jnp.float32)


def split(x):
    high = x.astype(jnp.bfloat16)
    return high, (x - high.astype(jnp.float32)).astype(jnp.bfloat16)


def times_parts(a, high, low, dims):
    a_high, a_low = split(a)
    rank = a.shape[0]
    both = dot16(jnp.concatenate([a_high, a_low], axis=0), high, dims)
    return both[:rank] + both[rank:] + dot16(a_high, low, dims)


def gram_of(left_t):
    rank = left_t.shape[0]
    high, rest = left_t.astype(jnp.bfloat16), None
    rest = left_t - high.astype(jnp.float32)
    middle = rest.astype(jnp.bfloat16)
    low = (rest - middle.astype(jnp.float32)).astype(jnp.bfloat16)
    parts = jnp.concatenate([high, middle, low], axis=0)
    grid = dot16(parts, parts, NT)
    rows = grid[:rank] + grid[rank : 2 * rank] + grid[2 * rank :]
    return rows[:, :rank] + rows[:, rank : 2 * rank] + rows[:, 2 * rank :]


def inverse_lower(gram):
    rank = gram.shape[0]
    count = rank // SUBLANES
    row_id = lax.broadcasted_iota(jnp.int32, (rank, LANES), 0)
    lane_id = lax.broadcasted_iota(jnp.int32, (rank, LANES), 1)
    unit = (lane_id == row_id + rank).astype(jnp.float32)
    work = jnp.concatenate([gram, unit[:, rank:]], axis=1)
    tiles = [work[q * SUBLANES : (q + 1) * SUBLANES] for q in range(count)]
    tile_row = row_id[:SUBLANES]
    done = []
    for g in range(count):
        spread = [
            [jnp.broadcast_to(tiles[q][:, k : k + 1], (SUBLANES, LANES)) for q in range(g, count)]
            for k in range(g * SUBLANES, (g + 1) * SUBLANES)
        ]
        out = tiles[g]
        for j in range(SUBLANES):
            scale = lax.rsqrt(spread[j][0][j : j + 1])
            row = tiles[g][j : j + 1] * scale
            out = jnp.where(tile_row == j, row, out)
            column = [part * scale for part in spread[j]]
            for k in range(j + 1, SUBLANES):
                cross = spread[k][0][j : j + 1] * scale
                spread[k] = [part - c * cross for part, c in zip(spread[k], column)]
            for q in range(g, count):
                tiles[q] = tiles[q] - column[q - g] * row
        done.append(out)
    return jnp.concatenate(done, axis=0)[:, rank : 2 * rank]


def step_kernel(
    reps,
    tps,
    grad_hbm,
    feed_hbm,
    warm_hbm,
    mom_hbm,
    master_hbm,
    vgrad_hbm,
    comb_ref,
    ortho_ref,
    right_ref,
    base_ref,
    vsum_ref,
    grad_ref,
    feed_ref,
    warm_ref,
    mom_ref,
    master_ref,
    vgrad_ref,
    load_sem,
    pair_send,
    pair_recv,
    line_send,
    line_recv,
    base_all,
    tp_send,
    tp_recv,
    left_all,
    piece_send,
    piece_recv,
    right_all,
    vec_all,
    pair_ss,
    pair_rs,
    line_ss,
    line_rs,
    base_ss,
    base_rs,
    fwd_ss,
    fwd_rs,
    tp_ss,
    tp_rs,
    left_ss,
    left_rs,
    piece_ss,
    piece_rs,
    right_ss,
    right_rs,
    vec_ss,
    vec_rs,
):
    me = lax.axis_index("rep")
    col = lax.axis_index("tp")
    lines = reps // 2
    far, near = me // 2, me % 2
    partner = far * 2 + (1 - near)
    rows, cols = mom_ref.shape
    rank = warm_ref.shape[0]
    half = rank // SUBLANES

    def rep_peer(k):
        return lax.rem(me + k, reps)

    def tp_peer(k):
        return lax.rem(col + k, tps)

    def line_at(d):
        return lax.rem(far + d, lines)

    def send(src, dst, ss, rs, peer):
        copy = pltpu.make_async_remote_copy(
            src_ref=src, dst_ref=dst, send_sem=ss, recv_sem=rs,
            device_id=peer, device_id_type=pl.DeviceIdType.MESH,
        )
        copy.start()
        sent.append(copy)
        return copy

    sent = []
    loads = []
    for i, (src, dst) in enumerate(
        (
            (grad_hbm, grad_ref),
            (feed_hbm, feed_ref),
            (mom_hbm, mom_ref),
            (master_hbm, master_ref),
            (warm_hbm, warm_ref),
            (vgrad_hbm, vgrad_ref),
        )
    ):
        loads.append(pltpu.make_async_copy(src, dst, load_sem.at[i]))
        loads[i].start()

    barrier = pltpu.get_barrier_semaphore()
    for k in range(1, reps):
        pl.semaphore_signal(barrier, inc=1, device_id={"rep": rep_peer(k)}, device_id_type=pl.DeviceIdType.MESH)
    for k in range(1, tps):
        pl.semaphore_signal(barrier, inc=1, device_id={"tp": tp_peer(k)}, device_id_type=pl.DeviceIdType.MESH)

    def combined_block(owner):
        at = pl.ds(pl.multiple_of(owner * rows, rows), rows)
        block = grad_ref[at, :].astype(jnp.float32) + feed_ref[at, :]
        comb_ref[at, :] = block
        return block

    order = list(range(1, lines)) + [0]
    loads[0].wait()
    loads[1].wait()
    for d in order:
        pair_send[d] = combined_block(line_at(d) * 2 + (1 - near)).astype(jnp.bfloat16)
    pl.semaphore_wait(barrier, reps - 1 + tps - 1)

    pairs = {}
    for d in order:
        pairs[d] = send(pair_send.at[d], pair_recv.at[d], pair_ss.at[d], pair_rs.at[d], {"rep": partner})
    for copy in loads[2:]:
        copy.wait()
    base_all[me] = (master_ref[...] - (LEARN_RATE * MOMENTUM_RATE) * mom_ref[...]).astype(jnp.bfloat16)
    vec_all[me] = vgrad_ref[...]
    line_copies = []
    for d in range(1, lines):
        mine = combined_block(line_at(d) * 2 + near)
        pairs[d].wait_recv()
        line_send[d] = (mine + pair_recv[d].astype(jnp.float32)).astype(jnp.bfloat16)
        line_copies.append(
            send(line_send.at[d], line_recv.at[d], line_ss.at[d], line_rs.at[d], {"rep": line_at(d) * 2 + near})
        )
    base_copies = [None]
    for d in range(1, lines):
        base_copies.append(
            send(base_all.at[me], base_all.at[me], base_ss.at[d], base_rs.at[d], {"rep": line_at(d) * 2 + near})
        )
    fwd_copies = [send(base_all.at[me], base_all.at[me], fwd_ss.at[0], fwd_rs.at[0], {"rep": partner})]
    vec_copies = []
    for k in range(1, reps):
        vec_copies.append(send(vec_all.at[me], vec_all.at[me], vec_ss.at[k], vec_rs.at[k], {"rep": rep_peer(k)}))
    total = combined_block(me)
    pairs[0].wait_recv()
    total = total + pair_recv[0].astype(jnp.float32)
    for d in range(1, lines):
        line_copies[d - 1].wait_recv()
        total = total + line_recv[d].astype(jnp.float32)
    sum_high, sum_low = split(total)

    def left_total(phase, factor_t):
        part = times_parts(factor_t, sum_high, sum_low, NT)
        tp_send[phase] = part
        copies = []
        for k in range(1, tps):
            copies.append(
                send(tp_send.at[phase], tp_recv.at[phase, k], tp_ss.at[phase, k], tp_rs.at[phase, k], {"tp": tp_peer(k)})
            )
        for k in range(1, tps):
            copies[k - 1].wait_recv()
            part = part + tp_recv[phase, k]
        return part

    def right_total(phase, left_t):
        left_all[phase, me] = left_t
        right_t = times_parts(left_t, sum_high, sum_low, NN)
        for s in range(cols // LANES):
            for q in range(half):
                piece_send[phase, s * half + q] = right_t[
                    q * SUBLANES : (q + 1) * SUBLANES, s * LANES : (s + 1) * LANES
                ]
        pieces, lefts, rights = [], [], []
        for k in range(1, reps):
            pieces.append(
                send(
                    piece_send.at[phase, rep_peer(k)], piece_recv.at[phase, k],
                    piece_ss.at[phase, k], piece_rs.at[phase, k], {"rep": rep_peer(k)},
                )
            )
        for k in range(1, reps):
            lefts.append(
                send(
                    left_all.at[phase, me], left_all.at[phase, me],
                    left_ss.at[phase, k], left_rs.at[phase, k], {"rep": rep_peer(k)},
                )
            )
        piece = piece_send[phase, me]
        for k in range(1, reps):
            pieces[k - 1].wait_recv()
            piece = piece + piece_recv[phase, k]
        right_all[phase, me] = piece
        for k in range(1, reps):
            rights.append(
                send(
                    right_all.at[phase, me], right_all.at[phase, me],
                    right_ss.at[phase, k], right_rs.at[phase, k], {"rep": rep_peer(k)},
                )
            )
        for copy in lefts:
            copy.wait_recv()
        left_full = jnp.concatenate([left_all[phase, r] for r in range(reps)], axis=1)
        unlower = inverse_lower(gram_of(left_full))

        def finish():
            for copy in rights:
                copy.wait_recv()
            raw = jnp.concatenate(
                [
                    jnp.concatenate([right_all[phase, s * half + q] for q in range(half)], axis=0)
                    for s in range(cols // LANES)
                ],
                axis=1,
            )
            return jnp.dot(unlower, raw, precision=PRECISE, preferred_element_type=jnp.float32)

        return left_full, unlower, finish

    left_one = left_total(0, warm_ref[...])
    _, _, finish_one = right_total(0, left_one)
    right_one = finish_one()
    for d in range(1, lines):
        base_copies[d].wait_recv()
        slot = lax.rem(far + lines - d, lines) * 2 + near
        fwd_copies.append(send(base_all.at[slot], base_all.at[slot], fwd_ss.at[d], fwd_rs.at[d], {"rep": partner}))
    left_two = left_total(1, right_one)
    left_full, unlower, finish_two = right_total(1, left_two)
    un_high, un_low = split(unlower)
    left_high, left_low = split(left_full)
    ortho = dot16(
        jnp.concatenate([un_high, un_low, un_high], axis=1),
        jnp.concatenate([left_high, left_high, left_low], axis=0),
        NN,
    )
    ortho_high, ortho_low = split(ortho)
    ortho_cat = jnp.concatenate([ortho_high, ortho_low, ortho_high], axis=0)
    for r in range(reps):
        ortho_ref[r] = ortho_cat[:, r * rows : (r + 1) * rows].T

    for copy in vec_copies:
        copy.wait_recv()
    vec_sum = vec_all[0]
    for r in range(1, reps):
        vec_sum = vec_sum + vec_all[r]
    vsum_ref[...] = vec_sum
    for copy in fwd_copies:
        copy.wait_recv()
    for r in range(reps):
        base_ref[r] = base_all[r]
    for copy in sent[: len(sent) - (reps - 1)]:
        copy.wait_send()

    right_high, right_low = split(finish_two() / reps)
    right_ref[...] = jnp.concatenate([right_high, right_high, right_low], axis=0)
    for copy in sent[len(sent) - (reps - 1) :]:
        copy.wait_send()


def finish_kernel(
    reps,
    comb_ref,
    ortho_ref,
    right_ref,
    base_ref,
    vsum_ref,
    mom_hbm,
    master_hbm,
    vpar_hbm,
    vmom_hbm,
    new_feed_hbm,
    new_mom_hbm,
    new_master_hbm,
    weight_hbm,
    new_vpar_hbm,
    new_vmom_hbm,
    mom_ref,
    master_ref,
    vpar_ref,
    vmom_ref,
    feed_ref,
    weight_ref,
    load_sem,
    feed_sem,
    weight_sem,
    out_sem,
):
    me = lax.axis_index("rep")
    rows = mom_ref.shape[0]
    loads = []
    for i, (src, dst) in enumerate(
        ((mom_hbm, mom_ref), (master_hbm, master_ref), (vpar_hbm, vpar_ref), (vmom_hbm, vmom_ref))
    ):
        loads.append(pltpu.make_async_copy(src, dst, load_sem.at[i]))
        loads[i].start()
    stores = []

    def store(src, dst, sem):
        stores.append(pltpu.make_async_copy(src, dst, sem))
        stores[-1].start()

    right = right_ref[...]
    for r in range(reps):
        at = pl.ds(r * rows, rows)
        approx = dot16(ortho_ref[r], right, NN)
        feed_ref[at, :] = comb_ref[at, :] - approx
        store(feed_ref.at[at, :], new_feed_hbm.at[at, :], feed_sem.at[r])
        weight_ref[at, :] = (base_ref[r].astype(jnp.float32) - LEARN_RATE * approx).astype(jnp.bfloat16)
        store(weight_ref.at[at, :], weight_hbm.at[at, :], weight_sem.at[r])
    own = dot16(ortho_ref[me], right, NN)
    for copy in loads:
        copy.wait()
    momentum = MOMENTUM_RATE * mom_ref[...] + own
    mom_ref[...] = momentum
    store(mom_ref, new_mom_hbm, out_sem.at[0])
    master_ref[...] = master_ref[...] - LEARN_RATE * momentum
    store(master_ref, new_master_hbm, out_sem.at[1])
    for c in range(vsum_ref.shape[1] // LANES):
        at = pl.ds(c * LANES, LANES)
        vec = MOMENTUM_RATE * vmom_ref[at] + vsum_ref[0, at] / reps
        vmom_ref[at] = vec
        vpar_ref[at] = vpar_ref[at] - LEARN_RATE * vec
    store(vpar_ref, new_vpar_hbm, out_sem.at[2])
    store(vmom_ref, new_vmom_hbm, out_sem.at[3])
    for copy in stores:
        copy.wait()


def kernel_shards(
    reps, tps, gradients, feedback, warm_factor, momentum, master_owned, vector_grads, vector_params, vector_momentum
):
    rows, cols = momentum.shape
    rank = warm_factor.shape[1]
    vec = vector_params.shape[0]
    lines = reps // 2
    f32, bf16 = jnp.float32, jnp.bfloat16
    dma = pltpu.SemaphoreType.DMA
    vmem = pl.BlockSpec(memory_space=pltpu.VMEM)
    hbm = pl.BlockSpec(memory_space=pltpu.HBM)
    whole = feedback.shape[1:]
    shape = jax.ShapeDtypeStruct
    parts = pl.pallas_call(
        functools.partial(step_kernel, reps, tps),
        out_shape=(
            shape(whole, f32),
            shape((reps, rows, 3 * rank), bf16),
            shape((3 * rank, cols), bf16),
            shape((reps, rows, cols), bf16),
            shape((1, vec), f32),
        ),
        in_specs=[hbm] * 6,
        out_specs=(vmem,) * 5,
        scratch_shapes=[
            pltpu.VMEM(whole, bf16),
            pltpu.VMEM(whole, f32),
            pltpu.VMEM((rank, cols), f32),
            pltpu.VMEM((rows, cols), f32),
            pltpu.VMEM((rows, cols), f32),
            pltpu.VMEM((1, vec), f32),
            dma((6,)),
            pltpu.VMEM((lines, rows, cols), bf16),
            pltpu.VMEM((lines, rows, cols), bf16),
            pltpu.VMEM((lines, rows, cols), bf16),
            pltpu.VMEM((lines, rows, cols), bf16),
            pltpu.VMEM((reps, rows, cols), bf16),
            pltpu.VMEM((2, rank, rows), f32),
            pltpu.VMEM((2, tps, rank, rows), f32),
            pltpu.VMEM((2, reps, rank, rows), f32),
            pltpu.VMEM((2, reps, SUBLANES, LANES), f32),
            pltpu.VMEM((2, reps, SUBLANES, LANES), f32),
            pltpu.VMEM((2, reps, SUBLANES, LANES), f32),
            pltpu.VMEM((reps, 1, vec), f32),
            dma((lines,)), dma((lines,)),
            dma((lines,)), dma((lines,)),
            dma((lines,)), dma((lines,)),
            dma((lines,)), dma((lines,)),
            dma((2, tps)), dma((2, tps)),
            dma((2, reps)), dma((2, reps)),
            dma((2, reps)), dma((2, reps)),
            dma((2, reps)), dma((2, reps)),
            dma((reps,)), dma((reps,)),
        ],
        compiler_params=pltpu.CompilerParams(
            collective_id=0, has_side_effects=True, vmem_limit_bytes=40 * 1024 * 1024
        ),
    )(
        gradients[0], feedback[0], warm_factor.T, momentum, master_owned, vector_grads
    )
    outs = pl.pallas_call(
        functools.partial(finish_kernel, reps),
        out_shape=(
            shape(whole, f32),
            shape((rows, cols), f32),
            shape((rows, cols), f32),
            shape(whole, bf16),
            shape((vec,), f32),
            shape((vec,), f32),
        ),
        in_specs=[vmem] * 5 + [hbm] * 4,
        out_specs=(hbm,) * 6,
        scratch_shapes=[
            pltpu.VMEM((rows, cols), f32),
            pltpu.VMEM((rows, cols), f32),
            pltpu.VMEM((vec,), f32),
            pltpu.VMEM((vec,), f32),
            pltpu.VMEM(whole, f32),
            pltpu.VMEM(whole, bf16),
            dma((4,)), dma((reps,)), dma((reps,)), dma((4,)),
        ],
        compiler_params=pltpu.CompilerParams(vmem_limit_bytes=40 * 1024 * 1024),
    )(*parts, momentum, master_owned, vector_params, vector_momentum)
    return (outs[0][None],) + tuple(outs[1:])


def step(reps, tps, *arrays):
    rows, cols = arrays[3].shape
    rank = arrays[2].shape[1]
    pieces = (cols // LANES) * (rank // SUBLANES)
    if reps == pieces and reps % 2 == 0 and rows == LANES:
        return kernel_shards(reps, tps, *arrays)
    return shards(*arrays)


def solution(mesh):
    return jax.shard_map(
        functools.partial(step, mesh.shape["rep"], mesh.shape["tp"]),
        mesh=mesh,
        in_specs=(
            P("rep", None, "tp"),
            P("rep", None, "tp"),
            P("tp", None),
            P("rep", "tp"),
            P("rep", "tp"),
            P("rep", None),
            P(),
            P(),
        ),
        out_specs=(P("rep", None, "tp"), P("rep", "tp"), P("rep", "tp"), P(None, "tp"), P(), P()),
        check_vma=False,
    )
```

```python
import functools

import jax
import jax.numpy as jnp
from jax import lax
from jax.experimental import pallas as pl
from jax.experimental.pallas import tpu as pltpu
from jax.sharding import PartitionSpec as P

PRECISE = lax.Precision.HIGHEST
MOMENTUM_RATE = 0.9
LEARN_RATE = 0.5


def left_factor(combined, factor):
    partial_terms = jnp.dot(combined, factor, precision=PRECISE)
    return lax.psum(partial_terms, ("rep", "tp"))


def orthonormal(left):
    gram = jnp.dot(left.T, left, precision=PRECISE)
    lower = jnp.linalg.cholesky(gram)
    return jax.scipy.linalg.solve_triangular(lower, left.T, lower=True).T


def right_terms(combined, ortho):
    return lax.dot_general(combined, ortho, (((0,), (0,)), ((), ())), precision=PRECISE)


def shards(
    gradients,
    feedback,
    warm_factor,
    momentum,
    master_owned,
    vector_grads,
    vector_params,
    vector_momentum,
):
    replicas = lax.axis_size("rep")
    combined = gradients[0].astype(jnp.float32) + feedback[0]
    vector_sum = lax.psum(vector_grads[0], "rep")
    left_one = left_factor(combined, warm_factor)
    ortho_one = orthonormal(left_one)
    right_one = lax.psum(right_terms(combined, ortho_one), "rep")
    left_two = left_factor(combined, right_one)
    ortho_two = orthonormal(left_two)
    right_two = lax.psum(right_terms(combined, ortho_two), "rep")
    approx = jnp.dot(ortho_two, right_two.T, precision=PRECISE) / replicas
    new_feedback = (combined - approx)[None]
    owned_rows = momentum.shape[0]
    row_start = lax.axis_index("rep") * owned_rows
    owned_approx = lax.dynamic_slice_in_dim(approx, row_start, owned_rows, 0)
    new_momentum = MOMENTUM_RATE * momentum + owned_approx
    new_master = master_owned - LEARN_RATE * new_momentum
    weight = lax.all_gather(new_master.astype(jnp.bfloat16), "rep", axis=0, tiled=True)
    new_vector_momentum = MOMENTUM_RATE * vector_momentum + vector_sum / replicas
    new_vector_params = vector_params - LEARN_RATE * new_vector_momentum
    return (new_feedback, new_momentum, new_master, weight, new_vector_params, new_vector_momentum)


LANES = 128
SUBLANES = 8
NT = (((1,), (1,)), ((), ()))
NN = (((1,), (0,)), ((), ()))
TN = (((0,), (0,)), ((), ()))


def dot16(a, b, dims):
    return lax.dot_general(a, b, dims, preferred_element_type=jnp.float32)


def split(x):
    high = x.astype(jnp.bfloat16)
    return high, (x - high.astype(jnp.float32)).astype(jnp.bfloat16)


def times_parts(a, high, low, dims):
    a_high, a_low = split(a)
    rank = a.shape[0]
    both = dot16(jnp.concatenate([a_high, a_low], axis=0), high, dims)
    return both[:rank] + both[rank:] + dot16(a_high, low, dims)


def gram_of(left_t):
    rank = left_t.shape[0]
    high = left_t.astype(jnp.bfloat16)
    rest = left_t - high.astype(jnp.float32)
    middle = rest.astype(jnp.bfloat16)
    low = (rest - middle.astype(jnp.float32)).astype(jnp.bfloat16)
    parts = jnp.concatenate([high, middle, low], axis=0)
    grid = dot16(parts, parts, NT)
    rows = grid[:rank] + grid[rank : 2 * rank] + grid[2 * rank :]
    return rows[:, :rank] + rows[:, rank : 2 * rank] + rows[:, 2 * rank :]


def stack_left(a):
    high, low = split(a)
    return jnp.concatenate([high, low, high], axis=1)


def stack_right(b):
    high, low = split(b)
    return jnp.concatenate([high, high, low], axis=0)


def pack_square(square):
    rank = square.shape[0]
    return jnp.concatenate([square[q : q + SUBLANES] for q in range(0, rank, SUBLANES)], axis=1)


def unpack_square(packed, rank):
    return jnp.concatenate([packed[:, q : q + rank] for q in range(0, LANES, rank)], axis=0)


def inverse_lower(gram):
    rank = gram.shape[0]
    count = rank // SUBLANES
    row_id = lax.broadcasted_iota(jnp.int32, (rank, LANES), 0)
    lane_id = lax.broadcasted_iota(jnp.int32, (rank, LANES), 1)
    unit = (lane_id == row_id + rank).astype(jnp.float32)
    work = jnp.concatenate([gram, unit[:, rank:]], axis=1)
    tiles = [work[q * SUBLANES : (q + 1) * SUBLANES] for q in range(count)]
    tile_row = row_id[:SUBLANES]
    done = []
    for g in range(count):
        spread = [
            [jnp.broadcast_to(tiles[q][:, k : k + 1], (SUBLANES, LANES)) for q in range(g, count)]
            for k in range(g * SUBLANES, (g + 1) * SUBLANES)
        ]
        out = tiles[g]
        for j in range(SUBLANES):
            scale = lax.rsqrt(spread[j][0][j : j + 1])
            row = tiles[g][j : j + 1] * scale
            out = jnp.where(tile_row == j, row, out)
            column = [part * scale for part in spread[j]]
            for k in range(j + 1, SUBLANES):
                cross = spread[k][0][j : j + 1] * scale
                spread[k] = [part - c * cross for part, c in zip(spread[k], column)]
            for q in range(g, count):
                tiles[q] = tiles[q] - column[q - g] * row
        done.append(out)
    return jnp.concatenate(done, axis=0)[:, rank : 2 * rank]


def step_kernel(
    reps,
    tps,
    grad_hbm,
    feed_hbm,
    warm_hbm,
    mom_hbm,
    master_hbm,
    vgrad_hbm,
    ortho_hbm,
    right_hbm,
    base_hbm,
    vsum_hbm,
    ortho_ref,
    right_ref,
    vsum_ref,
    out_sem,
    grad_ref,
    feed_ref,
    warm_ref,
    mom_ref,
    master_ref,
    vgrad_ref,
    load_sem,
    pair_send,
    pair_recv,
    line_send,
    line_recv,
    base_all,
    tp_send,
    tp_recv,
    left_all,
    piece_send,
    piece_recv,
    right_all,
    vec_all,
    vec_tp,
    gram_all,
    pair_ss,
    pair_rs,
    line_ss,
    line_rs,
    base_ss,
    base_rs,
    fwd_ss,
    fwd_rs,
    tp_ss,
    tp_rs,
    left_ss,
    left_rs,
    piece_ss,
    piece_rs,
    right_ss,
    right_rs,
    vec_ss,
    vec_rs,
    vtp_ss,
    vtp_rs,
    gram_ss,
    gram_rs,
):
    me = lax.axis_index("rep")
    col = lax.axis_index("tp")
    lines = reps // 2
    far, near = me // 2, me % 2
    partner = far * 2 + (1 - near)
    rows, cols = mom_ref.shape
    rank = warm_ref.shape[0]
    half = rank // SUBLANES

    def rep_peer(k):
        return lax.rem(me + k, reps)

    def tp_peer(k):
        return lax.rem(col + k, tps)

    def line_at(d):
        return lax.rem(far + d, lines)

    def send(src, dst, ss, rs, peer):
        copy = pltpu.make_async_remote_copy(
            src_ref=src, dst_ref=dst, send_sem=ss, recv_sem=rs,
            device_id=peer, device_id_type=pl.DeviceIdType.MESH,
        )
        copy.start()
        sent.append(copy)
        return copy

    sent = []
    loads = []
    for i, (src, dst) in enumerate(
        (
            (grad_hbm, grad_ref),
            (feed_hbm, feed_ref),
            (mom_hbm, mom_ref),
            (master_hbm, master_ref),
            (warm_hbm, warm_ref),
            (vgrad_hbm, vgrad_ref),
        )
    ):
        loads.append(pltpu.make_async_copy(src, dst, load_sem.at[i]))
        loads[i].start()

    barrier = pltpu.get_barrier_semaphore()
    for k in range(1, reps):
        pl.semaphore_signal(barrier, inc=1, device_id={"rep": rep_peer(k)}, device_id_type=pl.DeviceIdType.MESH)
    for k in range(1, tps):
        pl.semaphore_signal(barrier, inc=1, device_id={"tp": tp_peer(k)}, device_id_type=pl.DeviceIdType.MESH)

    def combined_block(owner):
        at = pl.ds(pl.multiple_of(owner * rows, rows), rows)
        return grad_ref[at, :].astype(jnp.float32) + feed_ref[at, :]

    order = list(range(1, lines)) + [0]
    loads[0].wait()
    loads[1].wait()
    for d in order:
        pair_send[d] = combined_block(line_at(d) * 2 + (1 - near)).astype(jnp.bfloat16)
    pl.semaphore_wait(barrier, reps - 1 + tps - 1)

    pairs = {}
    for d in order:
        pairs[d] = send(pair_send.at[d], pair_recv.at[d], pair_ss.at[d], pair_rs.at[d], {"rep": partner})
    for copy in loads[2:]:
        copy.wait()
    base_all[me] = (master_ref[...] - (LEARN_RATE * MOMENTUM_RATE) * mom_ref[...]).astype(jnp.bfloat16)
    quarter = vgrad_ref.shape[1] // tps
    vec_all[me] = vgrad_ref[:, pl.ds(pl.multiple_of(col * quarter, LANES), quarter)]
    base_copies = [None]

    def send_base(d):
        base_copies.append(
            send(base_all.at[me], base_all.at[me], base_ss.at[d], base_rs.at[d], {"rep": line_at(d) * 2 + near})
        )

    for d in range(1, lines - 1):
        send_base(d)
    line_copies = []
    for d in range(1, lines):
        mine = combined_block(line_at(d) * 2 + near)
        pairs[d].wait_recv()
        line_send[d] = (mine + pair_recv[d].astype(jnp.float32)).astype(jnp.bfloat16)
        line_copies.append(
            send(line_send.at[d], line_recv.at[d], line_ss.at[d], line_rs.at[d], {"rep": line_at(d) * 2 + near})
        )
    total = combined_block(me)
    pairs[0].wait_recv()
    total = total + pair_recv[0].astype(jnp.float32)
    for d in range(1, lines):
        line_copies[d - 1].wait_recv()
        total = total + line_recv[d].astype(jnp.float32)
    sum_high, sum_low = split(total)

    def left_total(phase, factor_t, meanwhile):
        part = times_parts(factor_t, sum_high, sum_low, NT)
        tp_send[phase] = part
        copies = []
        for k in range(1, tps):
            copies.append(
                send(tp_send.at[phase], tp_recv.at[phase, k], tp_ss.at[phase, k], tp_rs.at[phase, k], {"tp": tp_peer(k)})
            )
        meanwhile()
        for k in range(1, tps):
            copies[k - 1].wait_recv()
            part = part + tp_recv[phase, k]
        return part

    def right_total(phase, left_t):
        gram_all[phase, me] = pack_square(gram_of(left_t))
        right_t = times_parts(left_t, sum_high, sum_low, NN)
        for s in range(cols // LANES):
            for q in range(half):
                piece_send[phase, s * half + q] = right_t[
                    q * SUBLANES : (q + 1) * SUBLANES, s * LANES : (s + 1) * LANES
                ]
        pieces, grams, rights = [], [], []
        for k in range(1, reps):
            pieces.append(
                send(
                    piece_send.at[phase, rep_peer(k)], piece_recv.at[phase, k],
                    piece_ss.at[phase, k], piece_rs.at[phase, k], {"rep": rep_peer(k)},
                )
            )
        for k in range(1, reps):
            grams.append(
                send(
                    gram_all.at[phase, me], gram_all.at[phase, me],
                    gram_ss.at[phase, k], gram_rs.at[phase, k], {"rep": rep_peer(k)},
                )
            )
        piece = piece_send[phase, me]
        for k in range(1, reps):
            pieces[k - 1].wait_recv()
            piece = piece + piece_recv[phase, k]
        right_all[phase, me] = piece
        for k in range(1, reps):
            rights.append(
                send(
                    right_all.at[phase, me], right_all.at[phase, me],
                    right_ss.at[phase, k], right_rs.at[phase, k], {"rep": rep_peer(k)},
                )
            )
        lefts = []
        if phase == 1:
            left_all[me] = left_t
            for k in range(1, reps):
                lefts.append(
                    send(left_all.at[me], left_all.at[me], left_ss.at[k], left_rs.at[k], {"rep": rep_peer(k)})
                )
        for copy in grams:
            copy.wait_recv()
        gram = gram_all[phase, 0]
        for r in range(1, reps):
            gram = gram + gram_all[phase, r]
        unlower = stack_left(inverse_lower(unpack_square(gram, rank)))

        def finish():
            for copy in rights:
                copy.wait_recv()
            raw = jnp.concatenate(
                [
                    jnp.concatenate([right_all[phase, s * half + q] for q in range(half)], axis=0)
                    for s in range(cols // LANES)
                ],
                axis=1,
            )
            return dot16(unlower, stack_right(raw), NN)

        return unlower, lefts, finish

    def forward(d):
        if d:
            base_copies[d].wait_recv()
        slot = lax.rem(far + lines - d, lines) * 2 + near
        fwd_copies.append(send(base_all.at[slot], base_all.at[slot], fwd_ss.at[d], fwd_rs.at[d], {"rep": partner}))

    fwd_copies, vec_copies, vtp_copies = [], [], []

    def during_one():
        send_base(lines - 1)
        for k in range(1, reps):
            vec_copies.append(send(vec_all.at[me], vec_all.at[me], vec_ss.at[k], vec_rs.at[k], {"rep": rep_peer(k)}))
        forward(0)
        for d in range(1, lines - 2):
            forward(d)

    def during_two():
        for copy in vec_copies:
            copy.wait_recv()
        vec_sum = vec_all[0]
        for r in range(1, reps):
            vec_sum = vec_sum + vec_all[r]
        vec_tp[col] = vec_sum
        for k in range(1, tps):
            vtp_copies.append(send(vec_tp.at[col], vec_tp.at[col], vtp_ss.at[k], vtp_rs.at[k], {"tp": tp_peer(k)}))
        for d in range(max(1, lines - 2), lines):
            forward(d)

    left_one = left_total(0, warm_ref[...], during_one)
    _, _, finish_one = right_total(0, left_one)
    left_two = left_total(1, finish_one(), during_two)
    unlower, lefts, finish_two = right_total(1, left_two)

    stores = []

    def store(src, dst):
        stores.append(pltpu.make_async_copy(src, dst, out_sem.at[len(stores)]))
        stores[-1].start()

    for copy in vtp_copies:
        copy.wait_recv()
    for t in range(tps):
        vsum_ref[:, t * quarter : (t + 1) * quarter] = vec_tp[t]
    store(vsum_ref, vsum_hbm)
    for copy in fwd_copies:
        copy.wait_recv()
    store(base_all, base_hbm)
    for copy in lefts:
        copy.wait_recv()
    for r in range(reps):
        ortho = dot16(unlower, stack_right(left_all[r]), NN)
        ortho_high, ortho_low = split(ortho)
        ortho_ref[r] = jnp.concatenate([ortho_high, ortho_low, ortho_high], axis=0).T
    store(ortho_ref, ortho_hbm)
    right_ref[...] = stack_right(finish_two() / reps)
    store(right_ref, right_hbm)
    for copy in sent:
        copy.wait_send()
    for copy in stores:
        copy.wait()


def finish_kernel(
    reps,
    grad_hbm,
    old_feed_hbm,
    ortho_hbm,
    right_hbm,
    base_hbm,
    vsum_hbm,
    mom_hbm,
    master_hbm,
    vpar_hbm,
    vmom_hbm,
    new_feed_hbm,
    new_mom_hbm,
    new_master_hbm,
    weight_hbm,
    new_vpar_hbm,
    new_vmom_hbm,
    grad_ref,
    old_feed_ref,
    ortho_ref,
    right_ref,
    base_ref,
    vsum_ref,
    mom_ref,
    master_ref,
    vpar_ref,
    vmom_ref,
    feed_ref,
    weight_ref,
    load_sem,
    chunk_sem,
    feed_sem,
    weight_sem,
    out_sem,
):
    me = lax.axis_index("rep")
    rows = mom_ref.shape[0]
    loads, chunks = [], []

    def load(src, dst, sem):
        copy = pltpu.make_async_copy(src, dst, sem)
        copy.start()
        return copy

    loads.append(load(right_hbm, right_ref, load_sem.at[0]))
    for r in range(reps):
        at = pl.ds(r * rows, rows)
        chunks.append(
            (
                load(ortho_hbm.at[r], ortho_ref.at[r], chunk_sem.at[0, r]),
                load(grad_hbm.at[at, :], grad_ref.at[at, :], chunk_sem.at[1, r]),
                load(old_feed_hbm.at[at, :], old_feed_ref.at[at, :], chunk_sem.at[2, r]),
                load(base_hbm.at[r], base_ref.at[r], chunk_sem.at[3, r]),
            )
        )
    for src, dst in (
        (vsum_hbm, vsum_ref),
        (mom_hbm, mom_ref),
        (master_hbm, master_ref),
        (vpar_hbm, vpar_ref),
        (vmom_hbm, vmom_ref),
    ):
        loads.append(load(src, dst, load_sem.at[len(loads)]))
    stores = []

    def store(src, dst, sem):
        stores.append(pltpu.make_async_copy(src, dst, sem))
        stores[-1].start()

    loads[0].wait()
    right = right_ref[...]
    for r in range(reps):
        at = pl.ds(r * rows, rows)
        for copy in chunks[r]:
            copy.wait()
        approx = dot16(ortho_ref[r], right, NN)
        feed_ref[at, :] = grad_ref[at, :].astype(jnp.float32) + old_feed_ref[at, :] - approx
        store(feed_ref.at[at, :], new_feed_hbm.at[at, :], feed_sem.at[r])
        weight_ref[at, :] = (base_ref[r].astype(jnp.float32) - LEARN_RATE * approx).astype(jnp.bfloat16)
        store(weight_ref.at[at, :], weight_hbm.at[at, :], weight_sem.at[r])
    own = dot16(ortho_ref[me], right, NN)
    for copy in loads[1:]:
        copy.wait()
    momentum = MOMENTUM_RATE * mom_ref[...] + own
    mom_ref[...] = momentum
    store(mom_ref, new_mom_hbm, out_sem.at[0])
    master_ref[...] = master_ref[...] - LEARN_RATE * momentum
    store(master_ref, new_master_hbm, out_sem.at[1])
    for c in range(vsum_ref.shape[1] // LANES):
        at = pl.ds(c * LANES, LANES)
        vec = MOMENTUM_RATE * vmom_ref[at] + vsum_ref[0, at] / reps
        vmom_ref[at] = vec
        vpar_ref[at] = vpar_ref[at] - LEARN_RATE * vec
    store(vpar_ref, new_vpar_hbm, out_sem.at[2])
    store(vmom_ref, new_vmom_hbm, out_sem.at[3])
    for copy in stores:
        copy.wait()


def kernel_shards(
    reps, tps, gradients, feedback, warm_factor, momentum, master_owned, vector_grads, vector_params, vector_momentum
):
    rows, cols = momentum.shape
    rank = warm_factor.shape[1]
    vec = vector_params.shape[0]
    lines = reps // 2
    f32, bf16 = jnp.float32, jnp.bfloat16
    dma = pltpu.SemaphoreType.DMA
    hbm = pl.BlockSpec(memory_space=pltpu.HBM)
    whole = feedback.shape[1:]
    shape = jax.ShapeDtypeStruct
    parts = pl.pallas_call(
        functools.partial(step_kernel, reps, tps),
        out_shape=(
            shape((reps, rows, 3 * rank), bf16),
            shape((3 * rank, cols), bf16),
            shape((reps, rows, cols), bf16),
            shape((1, vec), f32),
        ),
        in_specs=[hbm] * 6,
        out_specs=(hbm,) * 4,
        scratch_shapes=[
            pltpu.VMEM((reps, rows, 3 * rank), bf16),
            pltpu.VMEM((3 * rank, cols), bf16),
            pltpu.VMEM((1, vec), f32),
            dma((4,)),
            pltpu.VMEM(whole, bf16),
            pltpu.VMEM(whole, f32),
            pltpu.VMEM((rank, cols), f32),
            pltpu.VMEM((rows, cols), f32),
            pltpu.VMEM((rows, cols), f32),
            pltpu.VMEM((1, vec), f32),
            dma((6,)),
            pltpu.VMEM((lines, rows, cols), bf16),
            pltpu.VMEM((lines, rows, cols), bf16),
            pltpu.VMEM((lines, rows, cols), bf16),
            pltpu.VMEM((lines, rows, cols), bf16),
            pltpu.VMEM((reps, rows, cols), bf16),
            pltpu.VMEM((2, rank, rows), f32),
            pltpu.VMEM((2, tps, rank, rows), f32),
            pltpu.VMEM((reps, rank, rows), f32),
            pltpu.VMEM((2, reps, SUBLANES, LANES), f32),
            pltpu.VMEM((2, reps, SUBLANES, LANES), f32),
            pltpu.VMEM((2, reps, SUBLANES, LANES), f32),
            pltpu.VMEM((reps, 1, vec // tps), f32),
            pltpu.VMEM((tps, 1, vec // tps), f32),
            pltpu.VMEM((2, reps, SUBLANES, LANES), f32),
            dma((lines,)), dma((lines,)),
            dma((lines,)), dma((lines,)),
            dma((lines,)), dma((lines,)),
            dma((lines,)), dma((lines,)),
            dma((2, tps)), dma((2, tps)),
            dma((reps,)), dma((reps,)),
            dma((2, reps)), dma((2, reps)),
            dma((2, reps)), dma((2, reps)),
            dma((reps,)), dma((reps,)),
            dma((tps,)), dma((tps,)),
            dma((2, reps)), dma((2, reps)),
        ],
        compiler_params=pltpu.CompilerParams(
            collective_id=0, has_side_effects=True, vmem_limit_bytes=56 * 1024 * 1024
        ),
    )(
        gradients[0], feedback[0], warm_factor.T, momentum, master_owned, vector_grads
    )
    outs = pl.pallas_call(
        functools.partial(finish_kernel, reps),
        out_shape=(
            shape(whole, f32),
            shape((rows, cols), f32),
            shape((rows, cols), f32),
            shape(whole, bf16),
            shape((vec,), f32),
            shape((vec,), f32),
        ),
        in_specs=[hbm] * 10,
        out_specs=(hbm,) * 6,
        scratch_shapes=[
            pltpu.VMEM(whole, bf16),
            pltpu.VMEM(whole, f32),
            pltpu.VMEM((reps, rows, 3 * rank), bf16),
            pltpu.VMEM((3 * rank, cols), bf16),
            pltpu.VMEM((reps, rows, cols), bf16),
            pltpu.VMEM((1, vec), f32),
            pltpu.VMEM((rows, cols), f32),
            pltpu.VMEM((rows, cols), f32),
            pltpu.VMEM((vec,), f32),
            pltpu.VMEM((vec,), f32),
            pltpu.VMEM(whole, f32),
            pltpu.VMEM(whole, bf16),
            dma((6,)), dma((4, reps)), dma((reps,)), dma((reps,)), dma((4,)),
        ],
        compiler_params=pltpu.CompilerParams(vmem_limit_bytes=56 * 1024 * 1024),
    )(gradients[0], feedback[0], *parts, momentum, master_owned, vector_params, vector_momentum)
    return (outs[0][None],) + tuple(outs[1:])


def step(reps, tps, *arrays):
    rows, cols = arrays[3].shape
    rank = arrays[2].shape[1]
    pieces = (cols // LANES) * (rank // SUBLANES)
    quarter = arrays[5].shape[1] // tps
    if reps == pieces and reps % 2 == 0 and rows == LANES and quarter % LANES == 0 and rank * SUBLANES * 4 == 8 * LANES:
        return kernel_shards(reps, tps, *arrays)
    return shards(*arrays)


def solution(mesh):
    return jax.shard_map(
        functools.partial(step, mesh.shape["rep"], mesh.shape["tp"]),
        mesh=mesh,
        in_specs=(
            P("rep", None, "tp"),
            P("rep", None, "tp"),
            P("tp", None),
            P("rep", "tp"),
            P("rep", "tp"),
            P("rep", None),
            P(),
            P(),
        ),
        out_specs=(P("rep", None, "tp"), P("rep", "tp"), P("rep", "tp"), P(None, "tp"), P(), P()),
        check_vma=False,
    )
```

```python
import functools

import jax
import jax.numpy as jnp
from jax import lax
from jax.experimental import pallas as pl
from jax.experimental.pallas import tpu as pltpu
from jax.sharding import PartitionSpec as P

PRECISE = lax.Precision.HIGHEST
MOMENTUM_RATE = 0.9
LEARN_RATE = 0.5


def left_factor(combined, factor):
    partial_terms = jnp.dot(combined, factor, precision=PRECISE)
    return lax.psum(partial_terms, ("rep", "tp"))


def orthonormal(left):
    gram = jnp.dot(left.T, left, precision=PRECISE)
    lower = jnp.linalg.cholesky(gram)
    return jax.scipy.linalg.solve_triangular(lower, left.T, lower=True).T


def right_terms(combined, ortho):
    return lax.dot_general(combined, ortho, (((0,), (0,)), ((), ())), precision=PRECISE)


def shards(
    gradients,
    feedback,
    warm_factor,
    momentum,
    master_owned,
    vector_grads,
    vector_params,
    vector_momentum,
):
    replicas = lax.axis_size("rep")
    combined = gradients[0].astype(jnp.float32) + feedback[0]
    vector_sum = lax.psum(vector_grads[0], "rep")
    left_one = left_factor(combined, warm_factor)
    ortho_one = orthonormal(left_one)
    right_one = lax.psum(right_terms(combined, ortho_one), "rep")
    left_two = left_factor(combined, right_one)
    ortho_two = orthonormal(left_two)
    right_two = lax.psum(right_terms(combined, ortho_two), "rep")
    approx = jnp.dot(ortho_two, right_two.T, precision=PRECISE) / replicas
    new_feedback = (combined - approx)[None]
    owned_rows = momentum.shape[0]
    row_start = lax.axis_index("rep") * owned_rows
    owned_approx = lax.dynamic_slice_in_dim(approx, row_start, owned_rows, 0)
    new_momentum = MOMENTUM_RATE * momentum + owned_approx
    new_master = master_owned - LEARN_RATE * new_momentum
    weight = lax.all_gather(new_master.astype(jnp.bfloat16), "rep", axis=0, tiled=True)
    new_vector_momentum = MOMENTUM_RATE * vector_momentum + vector_sum / replicas
    new_vector_params = vector_params - LEARN_RATE * new_vector_momentum
    return (new_feedback, new_momentum, new_master, weight, new_vector_params, new_vector_momentum)


LANES = 128
SUBLANES = 8
NT = (((1,), (1,)), ((), ()))
NN = (((1,), (0,)), ((), ()))
TN = (((0,), (0,)), ((), ()))


def dot16(a, b, dims):
    return lax.dot_general(a, b, dims, preferred_element_type=jnp.float32)


def split(x):
    high = x.astype(jnp.bfloat16)
    return high, (x - high.astype(jnp.float32)).astype(jnp.bfloat16)


def times_parts(a, high, low, dims):
    a_high, a_low = split(a)
    rank = a.shape[0]
    both = dot16(jnp.concatenate([a_high, a_low], axis=0), high, dims)
    return both[:rank] + both[rank:] + dot16(a_high, low, dims)


def gram_of(left_t):
    rank = left_t.shape[0]
    high = left_t.astype(jnp.bfloat16)
    rest = left_t - high.astype(jnp.float32)
    middle = rest.astype(jnp.bfloat16)
    low = (rest - middle.astype(jnp.float32)).astype(jnp.bfloat16)
    parts = jnp.concatenate([high, middle, low], axis=0)
    grid = dot16(parts, parts, NT)
    rows = grid[:rank] + grid[rank : 2 * rank] + grid[2 * rank :]
    return rows[:, :rank] + rows[:, rank : 2 * rank] + rows[:, 2 * rank :]


def stack_left(a):
    high, low = split(a)
    return jnp.concatenate([high, low, high], axis=1)


def stack_right(b):
    high, low = split(b)
    return jnp.concatenate([high, high, low], axis=0)


def pack_square(square):
    rank = square.shape[0]
    return jnp.concatenate([square[q : q + SUBLANES] for q in range(0, rank, SUBLANES)], axis=1)


def unpack_square(packed, rank):
    return jnp.concatenate([packed[:, q : q + rank] for q in range(0, LANES, rank)], axis=0)


def inverse_lower(gram):
    rank = gram.shape[0]
    count = rank // SUBLANES
    row_id = lax.broadcasted_iota(jnp.int32, (rank, LANES), 0)
    lane_id = lax.broadcasted_iota(jnp.int32, (rank, LANES), 1)
    unit = (lane_id == row_id + rank).astype(jnp.float32)
    work = jnp.concatenate([gram, unit[:, rank:]], axis=1)
    tiles = [work[q * SUBLANES : (q + 1) * SUBLANES] for q in range(count)]
    tile_row = row_id[:SUBLANES]
    done = []
    for g in range(count):
        spread = [
            [jnp.broadcast_to(tiles[q][:, k : k + 1], (SUBLANES, LANES)) for q in range(g, count)]
            for k in range(g * SUBLANES, (g + 1) * SUBLANES)
        ]
        out = tiles[g]
        for j in range(SUBLANES):
            scale = lax.rsqrt(spread[j][0][j : j + 1])
            row = tiles[g][j : j + 1] * scale
            out = jnp.where(tile_row == j, row, out)
            column = [part * scale for part in spread[j]]
            for k in range(j + 1, SUBLANES):
                cross = spread[k][0][j : j + 1] * scale
                spread[k] = [part - c * cross for part, c in zip(spread[k], column)]
            for q in range(g, count):
                tiles[q] = tiles[q] - column[q - g] * row
        done.append(out)
    return jnp.concatenate(done, axis=0)[:, rank : 2 * rank]


def step_kernel(
    reps,
    tps,
    grad_hbm,
    feed_hbm,
    warm_hbm,
    mom_hbm,
    master_hbm,
    vgrad_hbm,
    ortho_hbm,
    right_hbm,
    base_hbm,
    vsum_hbm,
    ortho_ref,
    right_ref,
    vsum_ref,
    out_sem,
    grad_ref,
    feed_ref,
    warm_ref,
    mom_ref,
    master_ref,
    vgrad_ref,
    load_sem,
    pair_send,
    pair_recv,
    line_send,
    line_recv,
    base_all,
    tp_send,
    tp_recv,
    left_all,
    piece_send,
    piece_recv,
    right_all,
    vec_all,
    vec_tp,
    pair_ss,
    pair_rs,
    line_ss,
    line_rs,
    base_ss,
    base_rs,
    fwd_ss,
    fwd_rs,
    tp_ss,
    tp_rs,
    left_ss,
    left_rs,
    piece_ss,
    piece_rs,
    right_ss,
    right_rs,
    vec_ss,
    vec_rs,
    vtp_ss,
    vtp_rs,
):
    me = lax.axis_index("rep")
    col = lax.axis_index("tp")
    lines = reps // 2
    far, near = me // 2, me % 2
    partner = far * 2 + (1 - near)
    rows, cols = mom_ref.shape
    rank = warm_ref.shape[0]
    half = rank // SUBLANES

    def rep_peer(k):
        return lax.rem(me + k, reps)

    def tp_peer(k):
        return lax.rem(col + k, tps)

    def line_at(d):
        return lax.rem(far + d, lines)

    def send(src, dst, ss, rs, peer):
        copy = pltpu.make_async_remote_copy(
            src_ref=src, dst_ref=dst, send_sem=ss, recv_sem=rs,
            device_id=peer, device_id_type=pl.DeviceIdType.MESH,
        )
        copy.start()
        sent.append(copy)
        return copy

    sent = []
    loads = []
    for i, (src, dst) in enumerate(
        (
            (grad_hbm, grad_ref),
            (feed_hbm, feed_ref),
            (mom_hbm, mom_ref),
            (master_hbm, master_ref),
            (warm_hbm, warm_ref),
            (vgrad_hbm, vgrad_ref),
        )
    ):
        loads.append(pltpu.make_async_copy(src, dst, load_sem.at[i]))
        loads[i].start()

    barrier = pltpu.get_barrier_semaphore()
    for k in range(1, reps):
        pl.semaphore_signal(barrier, inc=1, device_id={"rep": rep_peer(k)}, device_id_type=pl.DeviceIdType.MESH)
    for k in range(1, tps):
        pl.semaphore_signal(barrier, inc=1, device_id={"tp": tp_peer(k)}, device_id_type=pl.DeviceIdType.MESH)

    def combined_block(owner):
        at = pl.ds(pl.multiple_of(owner * rows, rows), rows)
        return grad_ref[at, :].astype(jnp.float32) + feed_ref[at, :]

    order = list(range(1, lines)) + [0]
    loads[0].wait()
    loads[1].wait()
    for d in order:
        pair_send[d] = combined_block(line_at(d) * 2 + (1 - near)).astype(jnp.bfloat16)
    pl.semaphore_wait(barrier, reps - 1 + tps - 1)

    pairs = {}
    for d in order:
        pairs[d] = send(pair_send.at[d], pair_recv.at[d], pair_ss.at[d], pair_rs.at[d], {"rep": partner})
    for copy in loads[2:]:
        copy.wait()
    base_all[me] = (master_ref[...] - (LEARN_RATE * MOMENTUM_RATE) * mom_ref[...]).astype(jnp.bfloat16)
    quarter = vgrad_ref.shape[1] // tps
    vec_all[me] = vgrad_ref[:, pl.ds(pl.multiple_of(col * quarter, LANES), quarter)]
    base_copies = [None]

    def send_base(d):
        base_copies.append(
            send(base_all.at[me], base_all.at[me], base_ss.at[d], base_rs.at[d], {"rep": line_at(d) * 2 + near})
        )

    send_base(1)
    line_copies = []
    for d in range(1, lines):
        mine = combined_block(line_at(d) * 2 + near)
        pairs[d].wait_recv()
        line_send[d] = (mine + pair_recv[d].astype(jnp.float32)).astype(jnp.bfloat16)
        line_copies.append(
            send(line_send.at[d], line_recv.at[d], line_ss.at[d], line_rs.at[d], {"rep": line_at(d) * 2 + near})
        )
    total = combined_block(me)
    pairs[0].wait_recv()
    total = total + pair_recv[0].astype(jnp.float32)
    for d in range(1, lines):
        line_copies[d - 1].wait_recv()
        total = total + line_recv[d].astype(jnp.float32)
    sum_high, sum_low = split(total)

    def left_total(phase, factor_t, meanwhile):
        part = times_parts(factor_t, sum_high, sum_low, NT)
        tp_send[phase] = part
        copies = []
        for k in range(1, tps):
            copies.append(
                send(tp_send.at[phase], tp_recv.at[phase, k], tp_ss.at[phase, k], tp_rs.at[phase, k], {"tp": tp_peer(k)})
            )
        meanwhile()
        for k in range(1, tps):
            copies[k - 1].wait_recv()
            part = part + tp_recv[phase, k]
        return part

    def right_total(phase, left_t):
        packed = pack_square(gram_of(left_t))
        right_t = times_parts(left_t, sum_high, sum_low, NN)
        for s in range(cols // LANES):
            for q in range(half):
                piece_send[phase, s * half + q, :SUBLANES] = right_t[
                    q * SUBLANES : (q + 1) * SUBLANES, s * LANES : (s + 1) * LANES
                ]
                piece_send[phase, s * half + q, SUBLANES:] = packed
        pieces, rights = [], []
        for k in range(1, reps):
            pieces.append(
                send(
                    piece_send.at[phase, rep_peer(k)], piece_recv.at[phase, me],
                    piece_ss.at[phase, k], piece_rs.at[phase, k], {"rep": rep_peer(k)},
                )
            )
        piece_recv[phase, me] = piece_send[phase, me]
        for copy in pieces:
            copy.wait_recv()
        both = piece_recv[phase, 0]
        for r in range(1, reps):
            both = both + piece_recv[phase, r]
        right_all[phase, me] = both[:SUBLANES]
        for k in range(1, reps):
            rights.append(
                send(
                    right_all.at[phase, me], right_all.at[phase, me],
                    right_ss.at[phase, k], right_rs.at[phase, k], {"rep": rep_peer(k)},
                )
            )
        lefts = []
        if phase == 1:
            left_all[me] = left_t
            for k in range(1, reps):
                lefts.append(
                    send(left_all.at[me], left_all.at[me], left_ss.at[k], left_rs.at[k], {"rep": rep_peer(k)})
                )
        unlower = stack_left(inverse_lower(unpack_square(both[SUBLANES:], rank)))

        def finish():
            for copy in rights:
                copy.wait_recv()
            raw = jnp.concatenate(
                [
                    jnp.concatenate([right_all[phase, s * half + q] for q in range(half)], axis=0)
                    for s in range(cols // LANES)
                ],
                axis=1,
            )
            return dot16(unlower, stack_right(raw), NN)

        return unlower, lefts, finish

    def forward(d):
        if d:
            base_copies[d].wait_recv()
        slot = lax.rem(far + lines - d, lines) * 2 + near
        fwd_copies.append(send(base_all.at[slot], base_all.at[slot], fwd_ss.at[d], fwd_rs.at[d], {"rep": partner}))

    fwd_copies, vec_copies, vtp_copies = [], [], []

    def during_one():
        for d in range(2, lines):
            send_base(d)
        for k in range(1, reps):
            vec_copies.append(send(vec_all.at[me], vec_all.at[me], vec_ss.at[k], vec_rs.at[k], {"rep": rep_peer(k)}))
        forward(0)
        for d in range(1, lines - 2):
            forward(d)

    def during_two():
        for copy in vec_copies:
            copy.wait_recv()
        vec_sum = vec_all[0]
        for r in range(1, reps):
            vec_sum = vec_sum + vec_all[r]
        vec_tp[col] = vec_sum
        for k in range(1, tps):
            vtp_copies.append(send(vec_tp.at[col], vec_tp.at[col], vtp_ss.at[k], vtp_rs.at[k], {"tp": tp_peer(k)}))
        for d in range(max(1, lines - 2), lines):
            forward(d)

    left_one = left_total(0, warm_ref[...], during_one)
    _, _, finish_one = right_total(0, left_one)
    left_two = left_total(1, finish_one(), during_two)
    unlower, lefts, finish_two = right_total(1, left_two)

    stores = []

    def store(src, dst):
        stores.append(pltpu.make_async_copy(src, dst, out_sem.at[len(stores)]))
        stores[-1].start()

    for copy in vtp_copies:
        copy.wait_recv()
    for t in range(tps):
        vsum_ref[:, t * quarter : (t + 1) * quarter] = vec_tp[t]
    store(vsum_ref, vsum_hbm)
    for copy in fwd_copies:
        copy.wait_recv()
    store(base_all, base_hbm)
    for copy in lefts:
        copy.wait_recv()
    for r in range(reps):
        ortho = dot16(unlower, stack_right(left_all[r]), NN)
        ortho_high, ortho_low = split(ortho)
        ortho_ref[r] = jnp.concatenate([ortho_high, ortho_low, ortho_high], axis=0).T
    store(ortho_ref, ortho_hbm)
    right_ref[...] = stack_right(finish_two() / reps)
    store(right_ref, right_hbm)
    for copy in sent:
        copy.wait_send()
    for copy in stores:
        copy.wait()


def finish_kernel(
    reps,
    grad_hbm,
    old_feed_hbm,
    ortho_hbm,
    right_hbm,
    base_hbm,
    vsum_hbm,
    mom_hbm,
    master_hbm,
    vpar_hbm,
    vmom_hbm,
    new_feed_hbm,
    new_mom_hbm,
    new_master_hbm,
    weight_hbm,
    new_vpar_hbm,
    new_vmom_hbm,
    grad_ref,
    old_feed_ref,
    ortho_ref,
    right_ref,
    base_ref,
    vsum_ref,
    mom_ref,
    master_ref,
    vpar_ref,
    vmom_ref,
    feed_ref,
    weight_ref,
    load_sem,
    chunk_sem,
    feed_sem,
    weight_sem,
    out_sem,
):
    me = lax.axis_index("rep")
    rows = mom_ref.shape[0]
    loads, chunks = [], []

    def load(src, dst, sem):
        copy = pltpu.make_async_copy(src, dst, sem)
        copy.start()
        return copy

    loads.append(load(right_hbm, right_ref, load_sem.at[0]))
    loads.append(load(ortho_hbm, ortho_ref, load_sem.at[1]))
    span = reps * rows // 2
    for h in range(2):
        at = pl.ds(h * span, span)
        chunks.append(
            (
                load(grad_hbm.at[at, :], grad_ref.at[at, :], chunk_sem.at[0, h]),
                load(old_feed_hbm.at[at, :], old_feed_ref.at[at, :], chunk_sem.at[1, h]),
            )
        )
    loads.append(load(base_hbm, base_ref, load_sem.at[2]))
    for src, dst in (
        (vsum_hbm, vsum_ref),
        (mom_hbm, mom_ref),
        (master_hbm, master_ref),
        (vpar_hbm, vpar_ref),
        (vmom_hbm, vmom_ref),
    ):
        loads.append(load(src, dst, load_sem.at[len(loads)]))
    stores = []

    def store(src, dst, sem):
        stores.append(pltpu.make_async_copy(src, dst, sem))
        stores[-1].start()

    loads[0].wait()
    loads[1].wait()
    right = right_ref[...]
    for r in range(reps):
        at = pl.ds(r * rows, rows)
        if r * rows % span == 0:
            for copy in chunks[r * rows // span]:
                copy.wait()
        if r == 0:
            loads[2].wait()
        approx = dot16(ortho_ref[r], right, NN)
        feed_ref[at, :] = grad_ref[at, :].astype(jnp.float32) + old_feed_ref[at, :] - approx
        weight_ref[at, :] = (base_ref[r].astype(jnp.float32) - LEARN_RATE * approx).astype(jnp.bfloat16)
        if (r + 1) * rows % span == 0:
            h = r * rows // span
            out = pl.ds(h * span, span)
            store(feed_ref.at[out, :], new_feed_hbm.at[out, :], feed_sem.at[h])
            store(weight_ref.at[out, :], weight_hbm.at[out, :], weight_sem.at[h])
    own = dot16(ortho_ref[me], right, NN)
    for copy in loads[3:]:
        copy.wait()
    momentum = MOMENTUM_RATE * mom_ref[...] + own
    mom_ref[...] = momentum
    store(mom_ref, new_mom_hbm, out_sem.at[0])
    master_ref[...] = master_ref[...] - LEARN_RATE * momentum
    store(master_ref, new_master_hbm, out_sem.at[1])
    for c in range(vsum_ref.shape[1] // LANES):
        at = pl.ds(c * LANES, LANES)
        vec = MOMENTUM_RATE * vmom_ref[at] + vsum_ref[0, at] / reps
        vmom_ref[at] = vec
        vpar_ref[at] = vpar_ref[at] - LEARN_RATE * vec
    store(vpar_ref, new_vpar_hbm, out_sem.at[2])
    store(vmom_ref, new_vmom_hbm, out_sem.at[3])
    for copy in stores:
        copy.wait()


def kernel_shards(
    reps, tps, gradients, feedback, warm_factor, momentum, master_owned, vector_grads, vector_params, vector_momentum
):
    rows, cols = momentum.shape
    rank = warm_factor.shape[1]
    vec = vector_params.shape[0]
    lines = reps // 2
    f32, bf16 = jnp.float32, jnp.bfloat16
    dma = pltpu.SemaphoreType.DMA
    hbm = pl.BlockSpec(memory_space=pltpu.HBM)
    whole = feedback.shape[1:]
    shape = jax.ShapeDtypeStruct
    parts = pl.pallas_call(
        functools.partial(step_kernel, reps, tps),
        out_shape=(
            shape((reps, rows, 3 * rank), bf16),
            shape((3 * rank, cols), bf16),
            shape((reps, rows, cols), bf16),
            shape((1, vec), f32),
        ),
        in_specs=[hbm] * 6,
        out_specs=(hbm,) * 4,
        scratch_shapes=[
            pltpu.VMEM((reps, rows, 3 * rank), bf16),
            pltpu.VMEM((3 * rank, cols), bf16),
            pltpu.VMEM((1, vec), f32),
            dma((4,)),
            pltpu.VMEM(whole, bf16),
            pltpu.VMEM(whole, f32),
            pltpu.VMEM((rank, cols), f32),
            pltpu.VMEM((rows, cols), f32),
            pltpu.VMEM((rows, cols), f32),
            pltpu.VMEM((1, vec), f32),
            dma((6,)),
            pltpu.VMEM((lines, rows, cols), bf16),
            pltpu.VMEM((lines, rows, cols), bf16),
            pltpu.VMEM((lines, rows, cols), bf16),
            pltpu.VMEM((lines, rows, cols), bf16),
            pltpu.VMEM((reps, rows, cols), bf16),
            pltpu.VMEM((2, rank, rows), f32),
            pltpu.VMEM((2, tps, rank, rows), f32),
            pltpu.VMEM((reps, rank, rows), f32),
            pltpu.VMEM((2, reps, 2 * SUBLANES, LANES), f32),
            pltpu.VMEM((2, reps, 2 * SUBLANES, LANES), f32),
            pltpu.VMEM((2, reps, SUBLANES, LANES), f32),
            pltpu.VMEM((reps, 1, vec // tps), f32),
            pltpu.VMEM((tps, 1, vec // tps), f32),
            dma((lines,)), dma((lines,)),
            dma((lines,)), dma((lines,)),
            dma((lines,)), dma((lines,)),
            dma((lines,)), dma((lines,)),
            dma((2, tps)), dma((2, tps)),
            dma((reps,)), dma((reps,)),
            dma((2, reps)), dma((2, reps)),
            dma((2, reps)), dma((2, reps)),
            dma((reps,)), dma((reps,)),
            dma((tps,)), dma((tps,)),
        ],
        compiler_params=pltpu.CompilerParams(
            collective_id=0, has_side_effects=True, vmem_limit_bytes=56 * 1024 * 1024
        ),
    )(
        gradients[0], feedback[0], warm_factor.T, momentum, master_owned, vector_grads
    )
    outs = pl.pallas_call(
        functools.partial(finish_kernel, reps),
        out_shape=(
            shape(whole, f32),
            shape((rows, cols), f32),
            shape((rows, cols), f32),
            shape(whole, bf16),
            shape((vec,), f32),
            shape((vec,), f32),
        ),
        in_specs=[hbm] * 10,
        out_specs=(hbm,) * 6,
        scratch_shapes=[
            pltpu.VMEM(whole, bf16),
            pltpu.VMEM(whole, f32),
            pltpu.VMEM((reps, rows, 3 * rank), bf16),
            pltpu.VMEM((3 * rank, cols), bf16),
            pltpu.VMEM((reps, rows, cols), bf16),
            pltpu.VMEM((1, vec), f32),
            pltpu.VMEM((rows, cols), f32),
            pltpu.VMEM((rows, cols), f32),
            pltpu.VMEM((vec,), f32),
            pltpu.VMEM((vec,), f32),
            pltpu.VMEM(whole, f32),
            pltpu.VMEM(whole, bf16),
            dma((8,)), dma((2, 2)), dma((2,)), dma((2,)), dma((4,)),
        ],
        compiler_params=pltpu.CompilerParams(vmem_limit_bytes=56 * 1024 * 1024),
    )(gradients[0], feedback[0], *parts, momentum, master_owned, vector_params, vector_momentum)
    return (outs[0][None],) + tuple(outs[1:])


def step(reps, tps, *arrays):
    rows, cols = arrays[3].shape
    rank = arrays[2].shape[1]
    pieces = (cols // LANES) * (rank // SUBLANES)
    quarter = arrays[5].shape[1] // tps
    if reps == pieces and reps % 2 == 0 and rows == LANES and quarter % LANES == 0 and rank * SUBLANES * 4 == 8 * LANES:
        return kernel_shards(reps, tps, *arrays)
    return shards(*arrays)


def solution(mesh):
    return jax.shard_map(
        functools.partial(step, mesh.shape["rep"], mesh.shape["tp"]),
        mesh=mesh,
        in_specs=(
            P("rep", None, "tp"),
            P("rep", None, "tp"),
            P("tp", None),
            P("rep", "tp"),
            P("rep", "tp"),
            P("rep", None),
            P(),
            P(),
        ),
        out_specs=(P("rep", None, "tp"), P("rep", "tp"), P("rep", "tp"), P(None, "tp"), P(), P()),
        check_vma=False,
    )
```

```python
import functools

import jax
import jax.numpy as jnp
from jax import lax
from jax.experimental import pallas as pl
from jax.experimental.pallas import tpu as pltpu
from jax.sharding import PartitionSpec as P

PRECISE = lax.Precision.HIGHEST
MOMENTUM_RATE = 0.9
LEARN_RATE = 0.5


def left_factor(combined, factor):
    partial_terms = jnp.dot(combined, factor, precision=PRECISE)
    return lax.psum(partial_terms, ("rep", "tp"))


def orthonormal(left):
    gram = jnp.dot(left.T, left, precision=PRECISE)
    lower = jnp.linalg.cholesky(gram)
    return jax.scipy.linalg.solve_triangular(lower, left.T, lower=True).T


def right_terms(combined, ortho):
    return lax.dot_general(combined, ortho, (((0,), (0,)), ((), ())), precision=PRECISE)


def shards(
    gradients,
    feedback,
    warm_factor,
    momentum,
    master_owned,
    vector_grads,
    vector_params,
    vector_momentum,
):
    replicas = lax.axis_size("rep")
    combined = gradients[0].astype(jnp.float32) + feedback[0]
    vector_sum = lax.psum(vector_grads[0], "rep")
    left_one = left_factor(combined, warm_factor)
    ortho_one = orthonormal(left_one)
    right_one = lax.psum(right_terms(combined, ortho_one), "rep")
    left_two = left_factor(combined, right_one)
    ortho_two = orthonormal(left_two)
    right_two = lax.psum(right_terms(combined, ortho_two), "rep")
    approx = jnp.dot(ortho_two, right_two.T, precision=PRECISE) / replicas
    new_feedback = (combined - approx)[None]
    owned_rows = momentum.shape[0]
    row_start = lax.axis_index("rep") * owned_rows
    owned_approx = lax.dynamic_slice_in_dim(approx, row_start, owned_rows, 0)
    new_momentum = MOMENTUM_RATE * momentum + owned_approx
    new_master = master_owned - LEARN_RATE * new_momentum
    weight = lax.all_gather(new_master.astype(jnp.bfloat16), "rep", axis=0, tiled=True)
    new_vector_momentum = MOMENTUM_RATE * vector_momentum + vector_sum / replicas
    new_vector_params = vector_params - LEARN_RATE * new_vector_momentum
    return (new_feedback, new_momentum, new_master, weight, new_vector_params, new_vector_momentum)


LANES = 128
SUBLANES = 8
NT = (((1,), (1,)), ((), ()))
NN = (((1,), (0,)), ((), ()))
TN = (((0,), (0,)), ((), ()))


def dot16(a, b, dims):
    return lax.dot_general(a, b, dims, preferred_element_type=jnp.float32)


def split(x):
    high = x.astype(jnp.bfloat16)
    return high, (x - high.astype(jnp.float32)).astype(jnp.bfloat16)


def times_parts(a, high, low, dims):
    a_high, a_low = split(a)
    rank = a.shape[0]
    both = dot16(jnp.concatenate([a_high, a_low], axis=0), high, dims)
    return both[:rank] + both[rank:] + dot16(a_high, low, dims)


def gram_of(left_t):
    rank = left_t.shape[0]
    high = left_t.astype(jnp.bfloat16)
    rest = left_t - high.astype(jnp.float32)
    middle = rest.astype(jnp.bfloat16)
    low = (rest - middle.astype(jnp.float32)).astype(jnp.bfloat16)
    parts = jnp.concatenate([high, middle, low], axis=0)
    grid = dot16(parts, parts, NT)
    rows = grid[:rank] + grid[rank : 2 * rank] + grid[2 * rank :]
    return rows[:, :rank] + rows[:, rank : 2 * rank] + rows[:, 2 * rank :]


def stack_left(a):
    high, low = split(a)
    return jnp.concatenate([high, low, high], axis=1)


def stack_right(b):
    high, low = split(b)
    return jnp.concatenate([high, high, low], axis=0)


def pack_square(square):
    rank = square.shape[0]
    return jnp.concatenate([square[q : q + SUBLANES] for q in range(0, rank, SUBLANES)], axis=1)


def unpack_square(packed, rank):
    return jnp.concatenate([packed[:, q : q + rank] for q in range(0, LANES, rank)], axis=0)


def inverse_lower(gram):
    rank = gram.shape[0]
    count = rank // SUBLANES
    row_id = lax.broadcasted_iota(jnp.int32, (rank, LANES), 0)
    lane_id = lax.broadcasted_iota(jnp.int32, (rank, LANES), 1)
    unit = (lane_id == row_id + rank).astype(jnp.float32)
    work = jnp.concatenate([gram, unit[:, rank:]], axis=1)
    tiles = [work[q * SUBLANES : (q + 1) * SUBLANES] for q in range(count)]
    tile_row = row_id[:SUBLANES]
    done = []
    for g in range(count):
        spread = [
            [jnp.broadcast_to(tiles[q][:, k : k + 1], (SUBLANES, LANES)) for q in range(g, count)]
            for k in range(g * SUBLANES, (g + 1) * SUBLANES)
        ]
        out = tiles[g]
        for j in range(SUBLANES):
            scale = lax.rsqrt(spread[j][0][j : j + 1])
            row = tiles[g][j : j + 1] * scale
            out = jnp.where(tile_row == j, row, out)
            column = [part * scale for part in spread[j]]
            for k in range(j + 1, SUBLANES):
                cross = spread[k][0][j : j + 1] * scale
                spread[k] = [part - c * cross for part, c in zip(spread[k], column)]
            for q in range(g, count):
                tiles[q] = tiles[q] - column[q - g] * row
        done.append(out)
    return jnp.concatenate(done, axis=0)[:, rank : 2 * rank]


def step_kernel(
    reps,
    tps,
    grad_hbm,
    feed_hbm,
    warm_hbm,
    mom_hbm,
    master_hbm,
    vgrad_hbm,
    ortho_hbm,
    right_hbm,
    base_hbm,
    vsum_hbm,
    ortho_ref,
    right_ref,
    vsum_ref,
    out_sem,
    grad_ref,
    feed_ref,
    warm_ref,
    mom_ref,
    master_ref,
    vgrad_ref,
    load_sem,
    pair_send,
    pair_recv,
    line_send,
    line_recv,
    base_all,
    tp_send,
    tp_recv,
    left_all,
    piece_send,
    piece_recv,
    right_all,
    vec_all,
    vec_tp,
    pair_ss,
    pair_rs,
    line_ss,
    line_rs,
    base_ss,
    base_rs,
    fwd_ss,
    fwd_rs,
    tp_ss,
    tp_rs,
    left_ss,
    left_rs,
    piece_ss,
    piece_rs,
    right_ss,
    right_rs,
    vec_ss,
    vec_rs,
    vtp_ss,
    vtp_rs,
):
    me = lax.axis_index("rep")
    col = lax.axis_index("tp")
    lines = reps // 2
    far, near = me // 2, me % 2
    partner = far * 2 + (1 - near)
    rows, cols = mom_ref.shape
    rank = warm_ref.shape[0]
    half = rank // SUBLANES

    def rep_peer(k):
        return lax.rem(me + k, reps)

    def tp_peer(k):
        return lax.rem(col + k, tps)

    def line_at(d):
        return lax.rem(far + d, lines)

    def send(src, dst, ss, rs, peer):
        copy = pltpu.make_async_remote_copy(
            src_ref=src, dst_ref=dst, send_sem=ss, recv_sem=rs,
            device_id=peer, device_id_type=pl.DeviceIdType.MESH,
        )
        copy.start()
        sent.append(copy)
        return copy

    sent = []
    loads = []
    for i, (src, dst) in enumerate(
        (
            (grad_hbm, grad_ref),
            (feed_hbm, feed_ref),
            (mom_hbm, mom_ref),
            (master_hbm, master_ref),
            (warm_hbm, warm_ref),
            (vgrad_hbm, vgrad_ref),
        )
    ):
        loads.append(pltpu.make_async_copy(src, dst, load_sem.at[i]))
        loads[i].start()

    barrier = pltpu.get_barrier_semaphore()
    for k in range(1, reps):
        pl.semaphore_signal(barrier, inc=1, device_id={"rep": rep_peer(k)}, device_id_type=pl.DeviceIdType.MESH)
    for k in range(1, tps):
        pl.semaphore_signal(barrier, inc=1, device_id={"tp": tp_peer(k)}, device_id_type=pl.DeviceIdType.MESH)

    def combined_block(owner):
        at = pl.ds(pl.multiple_of(owner * rows, rows), rows)
        return grad_ref[at, :].astype(jnp.float32) + feed_ref[at, :]

    order = list(range(1, lines)) + [0]
    loads[0].wait()
    loads[1].wait()
    for d in order:
        pair_send[d] = combined_block(line_at(d) * 2 + (1 - near)).astype(jnp.bfloat16)
    pl.semaphore_wait(barrier, reps - 1 + tps - 1)

    pairs = {}

    def send_pair(d):
        pairs[d] = send(pair_send.at[d], pair_recv.at[d], pair_ss.at[d], pair_rs.at[d], {"rep": partner})

    for d in order[:2]:
        send_pair(d)
    for copy in loads[2:]:
        copy.wait()
    base_all[me] = (master_ref[...] - (LEARN_RATE * MOMENTUM_RATE) * mom_ref[...]).astype(jnp.bfloat16)
    quarter = vgrad_ref.shape[1] // tps
    vec_all[me] = vgrad_ref[:, pl.ds(pl.multiple_of(col * quarter, LANES), quarter)]
    base_copies = [None]

    def send_base(d):
        base_copies.append(
            send(base_all.at[me], base_all.at[me], base_ss.at[d], base_rs.at[d], {"rep": line_at(d) * 2 + near})
        )

    line_copies = []
    for d in range(1, lines):
        mine = combined_block(line_at(d) * 2 + near)
        pairs[d].wait_recv()
        if d + 1 < lines:
            send_pair(order[d + 1])
        line_send[d] = (mine + pair_recv[d].astype(jnp.float32)).astype(jnp.bfloat16)
        line_copies.append(
            send(line_send.at[d], line_recv.at[d], line_ss.at[d], line_rs.at[d], {"rep": line_at(d) * 2 + near})
        )
    total = combined_block(me)
    pairs[0].wait_recv()
    total = total + pair_recv[0].astype(jnp.float32)
    for d in range(1, lines):
        line_copies[d - 1].wait_recv()
        total = total + line_recv[d].astype(jnp.float32)
    sum_high, sum_low = split(total)

    def left_total(phase, factor_t, meanwhile):
        part = times_parts(factor_t, sum_high, sum_low, NT)
        tp_send[phase] = part
        copies = []
        for k in range(1, tps):
            copies.append(
                send(tp_send.at[phase], tp_recv.at[phase, k], tp_ss.at[phase, k], tp_rs.at[phase, k], {"tp": tp_peer(k)})
            )
        meanwhile()
        for k in range(1, tps):
            copies[k - 1].wait_recv()
            part = part + tp_recv[phase, k]
        return part

    def right_total(phase, left_t):
        packed = pack_square(gram_of(left_t))
        right_t = times_parts(left_t, sum_high, sum_low, NN)
        for s in range(cols // LANES):
            for q in range(half):
                piece_send[phase, s * half + q, :SUBLANES] = right_t[
                    q * SUBLANES : (q + 1) * SUBLANES, s * LANES : (s + 1) * LANES
                ]
                piece_send[phase, s * half + q, SUBLANES:] = packed
        pieces, rights = [], []
        for k in range(1, reps):
            pieces.append(
                send(
                    piece_send.at[phase, rep_peer(k)], piece_recv.at[phase, me],
                    piece_ss.at[phase, k], piece_rs.at[phase, k], {"rep": rep_peer(k)},
                )
            )
        piece_recv[phase, me] = piece_send[phase, me]
        for copy in pieces:
            copy.wait_recv()
        both = piece_recv[phase, 0]
        for r in range(1, reps):
            both = both + piece_recv[phase, r]
        right_all[phase, me] = both[:SUBLANES]
        for k in range(1, reps):
            rights.append(
                send(
                    right_all.at[phase, me], right_all.at[phase, me],
                    right_ss.at[phase, k], right_rs.at[phase, k], {"rep": rep_peer(k)},
                )
            )
        lefts = []
        if phase == 1:
            left_all[me] = left_t
            for k in range(1, reps):
                lefts.append(
                    send(left_all.at[me], left_all.at[me], left_ss.at[k], left_rs.at[k], {"rep": rep_peer(k)})
                )
        unlower = stack_left(inverse_lower(unpack_square(both[SUBLANES:], rank)))

        def finish():
            for copy in rights:
                copy.wait_recv()
            raw = jnp.concatenate(
                [
                    jnp.concatenate([right_all[phase, s * half + q] for q in range(half)], axis=0)
                    for s in range(cols // LANES)
                ],
                axis=1,
            )
            return dot16(unlower, stack_right(raw), NN)

        return unlower, lefts, finish

    def forward(d):
        if d:
            base_copies[d].wait_recv()
        slot = lax.rem(far + lines - d, lines) * 2 + near
        fwd_copies.append(send(base_all.at[slot], base_all.at[slot], fwd_ss.at[d], fwd_rs.at[d], {"rep": partner}))

    fwd_copies, vec_copies, vtp_copies, early = [], [], [], []

    def during_one():
        for d in range(1, lines):
            send_base(d)
        for k in range(1, reps):
            vec_copies.append(send(vec_all.at[me], vec_all.at[me], vec_ss.at[k], vec_rs.at[k], {"rep": rep_peer(k)}))
        forward(0)
        for d in range(1, lines - 2):
            forward(d)

    def during_two():
        for copy in sent:
            if not any(copy is other for other in base_copies + fwd_copies):
                copy.wait_send()
                early.append(copy)
        for copy in vec_copies:
            copy.wait_recv()
        vec_sum = vec_all[0]
        for r in range(1, reps):
            vec_sum = vec_sum + vec_all[r]
        vec_tp[col] = vec_sum
        for k in range(1, tps):
            vtp_copies.append(send(vec_tp.at[col], vec_tp.at[col], vtp_ss.at[k], vtp_rs.at[k], {"tp": tp_peer(k)}))
        for d in range(max(1, lines - 2), lines):
            forward(d)

    left_one = left_total(0, warm_ref[...], during_one)
    _, _, finish_one = right_total(0, left_one)
    left_two = left_total(1, finish_one(), during_two)
    unlower, lefts, finish_two = right_total(1, left_two)

    stores = []

    def store(src, dst):
        stores.append(pltpu.make_async_copy(src, dst, out_sem.at[len(stores)]))
        stores[-1].start()

    for copy in vtp_copies:
        copy.wait_recv()
    for t in range(tps):
        vsum_ref[:, t * quarter : (t + 1) * quarter] = vec_tp[t]
    store(vsum_ref, vsum_hbm)
    for copy in fwd_copies:
        copy.wait_recv()
    store(base_all, base_hbm)
    for copy in lefts:
        copy.wait_recv()
    for r in range(reps):
        ortho = dot16(unlower, stack_right(left_all[r]), NN)
        ortho_high, ortho_low = split(ortho)
        ortho_ref[r] = jnp.concatenate([ortho_high, ortho_low, ortho_high], axis=0).T
    store(ortho_ref, ortho_hbm)
    right_ref[...] = stack_right(finish_two() / reps)
    store(right_ref, right_hbm)
    for copy in sent:
        if not any(copy is other for other in early):
            copy.wait_send()
    for copy in stores:
        copy.wait()


def finish_kernel(
    reps,
    grad_hbm,
    old_feed_hbm,
    ortho_hbm,
    right_hbm,
    base_hbm,
    vsum_hbm,
    mom_hbm,
    master_hbm,
    vpar_hbm,
    vmom_hbm,
    new_feed_hbm,
    new_mom_hbm,
    new_master_hbm,
    weight_hbm,
    new_vpar_hbm,
    new_vmom_hbm,
    grad_ref,
    old_feed_ref,
    ortho_ref,
    right_ref,
    base_ref,
    vsum_ref,
    mom_ref,
    master_ref,
    vpar_ref,
    vmom_ref,
    feed_ref,
    weight_ref,
    load_sem,
    chunk_sem,
    feed_sem,
    weight_sem,
    out_sem,
):
    me = lax.axis_index("rep")
    rows = mom_ref.shape[0]
    loads, chunks = [], []

    def load(src, dst, sem):
        copy = pltpu.make_async_copy(src, dst, sem)
        copy.start()
        return copy

    loads.append(load(right_hbm, right_ref, load_sem.at[0]))
    loads.append(load(ortho_hbm, ortho_ref, load_sem.at[1]))
    span = reps * rows // 2
    for h in range(2):
        at = pl.ds(h * span, span)
        chunks.append(
            (
                load(grad_hbm.at[at, :], grad_ref.at[at, :], chunk_sem.at[0, h]),
                load(old_feed_hbm.at[at, :], old_feed_ref.at[at, :], chunk_sem.at[1, h]),
            )
        )
    loads.append(load(base_hbm, base_ref, load_sem.at[2]))
    for src, dst in (
        (vsum_hbm, vsum_ref),
        (mom_hbm, mom_ref),
        (master_hbm, master_ref),
        (vpar_hbm, vpar_ref),
        (vmom_hbm, vmom_ref),
    ):
        loads.append(load(src, dst, load_sem.at[len(loads)]))
    stores = []

    def store(src, dst, sem):
        stores.append(pltpu.make_async_copy(src, dst, sem))
        stores[-1].start()

    loads[0].wait()
    loads[1].wait()
    right = right_ref[...]
    for r in range(reps):
        at = pl.ds(r * rows, rows)
        if r * rows % span == 0:
            for copy in chunks[r * rows // span]:
                copy.wait()
        if r == 0:
            loads[2].wait()
        approx = dot16(ortho_ref[r], right, NN)
        feed_ref[at, :] = grad_ref[at, :].astype(jnp.float32) + old_feed_ref[at, :] - approx
        weight_ref[at, :] = (base_ref[r].astype(jnp.float32) - LEARN_RATE * approx).astype(jnp.bfloat16)
        if (r + 1) * rows % span == 0:
            h = r * rows // span
            out = pl.ds(h * span, span)
            store(feed_ref.at[out, :], new_feed_hbm.at[out, :], feed_sem.at[h])
            store(weight_ref.at[out, :], weight_hbm.at[out, :], weight_sem.at[h])
    own = dot16(ortho_ref[me], right, NN)
    for copy in loads[3:]:
        copy.wait()
    momentum = MOMENTUM_RATE * mom_ref[...] + own
    mom_ref[...] = momentum
    store(mom_ref, new_mom_hbm, out_sem.at[0])
    master_ref[...] = master_ref[...] - LEARN_RATE * momentum
    store(master_ref, new_master_hbm, out_sem.at[1])
    for c in range(vsum_ref.shape[1] // LANES):
        at = pl.ds(c * LANES, LANES)
        vec = MOMENTUM_RATE * vmom_ref[at] + vsum_ref[0, at] / reps
        vmom_ref[at] = vec
        vpar_ref[at] = vpar_ref[at] - LEARN_RATE * vec
    store(vpar_ref, new_vpar_hbm, out_sem.at[2])
    store(vmom_ref, new_vmom_hbm, out_sem.at[3])
    for copy in stores:
        copy.wait()


def kernel_shards(
    reps, tps, gradients, feedback, warm_factor, momentum, master_owned, vector_grads, vector_params, vector_momentum
):
    rows, cols = momentum.shape
    rank = warm_factor.shape[1]
    vec = vector_params.shape[0]
    lines = reps // 2
    f32, bf16 = jnp.float32, jnp.bfloat16
    dma = pltpu.SemaphoreType.DMA
    hbm = pl.BlockSpec(memory_space=pltpu.HBM)
    whole = feedback.shape[1:]
    shape = jax.ShapeDtypeStruct
    parts = pl.pallas_call(
        functools.partial(step_kernel, reps, tps),
        out_shape=(
            shape((reps, rows, 3 * rank), bf16),
            shape((3 * rank, cols), bf16),
            shape((reps, rows, cols), bf16),
            shape((1, vec), f32),
        ),
        in_specs=[hbm] * 6,
        out_specs=(hbm,) * 4,
        scratch_shapes=[
            pltpu.VMEM((reps, rows, 3 * rank), bf16),
            pltpu.VMEM((3 * rank, cols), bf16),
            pltpu.VMEM((1, vec), f32),
            dma((4,)),
            pltpu.VMEM(whole, bf16),
            pltpu.VMEM(whole, f32),
            pltpu.VMEM((rank, cols), f32),
            pltpu.VMEM((rows, cols), f32),
            pltpu.VMEM((rows, cols), f32),
            pltpu.VMEM((1, vec), f32),
            dma((6,)),
            pltpu.VMEM((lines, rows, cols), bf16),
            pltpu.VMEM((lines, rows, cols), bf16),
            pltpu.VMEM((lines, rows, cols), bf16),
            pltpu.VMEM((lines, rows, cols), bf16),
            pltpu.VMEM((reps, rows, cols), bf16),
            pltpu.VMEM((2, rank, rows), f32),
            pltpu.VMEM((2, tps, rank, rows), f32),
            pltpu.VMEM((reps, rank, rows), f32),
            pltpu.VMEM((2, reps, 2 * SUBLANES, LANES), f32),
            pltpu.VMEM((2, reps, 2 * SUBLANES, LANES), f32),
            pltpu.VMEM((2, reps, SUBLANES, LANES), f32),
            pltpu.VMEM((reps, 1, vec // tps), f32),
            pltpu.VMEM((tps, 1, vec // tps), f32),
            dma((lines,)), dma((lines,)),
            dma((lines,)), dma((lines,)),
            dma((lines,)), dma((lines,)),
            dma((lines,)), dma((lines,)),
            dma((2, tps)), dma((2, tps)),
            dma((reps,)), dma((reps,)),
            dma((2, reps)), dma((2, reps)),
            dma((2, reps)), dma((2, reps)),
            dma((reps,)), dma((reps,)),
            dma((tps,)), dma((tps,)),
        ],
        compiler_params=pltpu.CompilerParams(
            collective_id=0, has_side_effects=True, vmem_limit_bytes=56 * 1024 * 1024
        ),
    )(
        gradients[0], feedback[0], warm_factor.T, momentum, master_owned, vector_grads
    )
    outs = pl.pallas_call(
        functools.partial(finish_kernel, reps),
        out_shape=(
            shape(whole, f32),
            shape((rows, cols), f32),
            shape((rows, cols), f32),
            shape(whole, bf16),
            shape((vec,), f32),
            shape((vec,), f32),
        ),
        in_specs=[hbm] * 10,
        out_specs=(hbm,) * 6,
        scratch_shapes=[
            pltpu.VMEM(whole, bf16),
            pltpu.VMEM(whole, f32),
            pltpu.VMEM((reps, rows, 3 * rank), bf16),
            pltpu.VMEM((3 * rank, cols), bf16),
            pltpu.VMEM((reps, rows, cols), bf16),
            pltpu.VMEM((1, vec), f32),
            pltpu.VMEM((rows, cols), f32),
            pltpu.VMEM((rows, cols), f32),
            pltpu.VMEM((vec,), f32),
            pltpu.VMEM((vec,), f32),
            pltpu.VMEM(whole, f32),
            pltpu.VMEM(whole, bf16),
            dma((8,)), dma((2, 2)), dma((2,)), dma((2,)), dma((4,)),
        ],
        compiler_params=pltpu.CompilerParams(vmem_limit_bytes=56 * 1024 * 1024),
    )(gradients[0], feedback[0], *parts, momentum, master_owned, vector_params, vector_momentum)
    return (outs[0][None],) + tuple(outs[1:])


def step(reps, tps, *arrays):
    rows, cols = arrays[3].shape
    rank = arrays[2].shape[1]
    pieces = (cols // LANES) * (rank // SUBLANES)
    quarter = arrays[5].shape[1] // tps
    if reps == pieces and reps % 2 == 0 and rows == LANES and quarter % LANES == 0 and rank * SUBLANES * 4 == 8 * LANES:
        return kernel_shards(reps, tps, *arrays)
    return shards(*arrays)


def solution(mesh):
    return jax.shard_map(
        functools.partial(step, mesh.shape["rep"], mesh.shape["tp"]),
        mesh=mesh,
        in_specs=(
            P("rep", None, "tp"),
            P("rep", None, "tp"),
            P("tp", None),
            P("rep", "tp"),
            P("rep", "tp"),
            P("rep", None),
            P(),
            P(),
        ),
        out_specs=(P("rep", None, "tp"), P("rep", "tp"), P("rep", "tp"), P(None, "tp"), P(), P()),
        check_vma=False,
    )
```
